128 devices in a mesh: row: 8 (over y, z_lo), col: 16 (over x, z_hi, core).
Axes of the slice: x: 4, y: 4, z: 4 (z_hi: 2, z_lo: 2; z = z_hi * 2 + z_lo), core: 2. Of those that a mesh axis runs over, the one named last changes fastest.
Arguments:
- factor: float32 [10240, 8192], P('row', 'col'), may hold values from -0.09375 to 0.09375
- inverse: float32 [2, 4096, 4096], P(None, 'row', 'col'), may hold values from -0.09375 to 0.09375
- rhs: float32 [10240, 1024], P('row'), may hold values from -6 to 6
Outputs:
- solved: float32 [10240, 1024], P('row')
The draws below stay inside these ranges and needn't reach their ends.
All inputs are finite; a program needn't handle non-finite values.
Results may differ from the reference program's by a relative error of at most 0.000078.
Values sent between devices are 32-bit elements; how exact they have to be, the bound alone decides.
A program may use at most 64 MiB of HBM per device.

```python
import jax
import jax.numpy as jnp
from jax import lax

NB = 256
R = 1024
BR_DEV = 5
PANEL = 4096
NWIN = 10240
N_ROW = 8
N_COL = 16


def steps_of(stream_key, extent, shards, low, top_value):
    gain = 1.0
    for position, shards_of in shards:
        draws = jax.random.uniform(jax.random.fold_in(jax.random.fold_in(stream_key, 6), position), (shards_of,), jnp.float32, low / len(shards), top_value / len(shards))
        gain = gain * jnp.repeat(jnp.exp(draws), extent[position] // shards_of).reshape((-1,) + (1,) * (len(extent) - 1 - position))
    return gain


def centred(rng, shape, scale, reach, pieces=(), kind=jnp.bfloat16):
    entries = scale * jax.random.normal(rng, shape, jnp.float32)
    if pieces:
        entries = entries * steps_of(rng, shape, pieces, -0.22, 0.18)
    return jnp.clip(entries, -reach, reach).astype(kind)


def setup_inputs(seed: int = 0) -> dict:
    seeds = jax.random.split(jax.random.key(seed), 4)
    factor = centred(seeds[0], (NWIN, 2 * PANEL), PANEL ** -0.5, 0.09375, ((0, 8), (1, 16)), jnp.float32)
    inverse = centred(seeds[1], (2, PANEL, PANEL), PANEL ** -0.5, 0.09375, ((1, 8), (2, 16)), jnp.float32)
    rhs = centred(seeds[2], (NWIN, R), 1.0, 6.0, ((0, 8),), jnp.float32)
    return {"factor": factor, "inverse": inverse, "rhs": rhs}


def to_global_rows(stored):
    width = stored.shape[-1]
    return stored.reshape(N_ROW, BR_DEV, NB, width).transpose(1, 0, 2, 3).reshape(NWIN, width)


def to_stored_rows(matrix):
    width = matrix.shape[-1]
    return matrix.reshape(BR_DEV, N_ROW, NB, width).transpose(1, 0, 2, 3).reshape(NWIN, width)


def matmul(left, right):
    return jnp.dot(left, right, precision=lax.Precision.HIGHEST, preferred_element_type=jnp.float32)


def reference(factor, inverse, rhs):
    upper = to_global_rows(factor)
    upper = upper.reshape(NWIN, N_COL, 2, NB).transpose(0, 2, 1, 3).reshape(NWIN, 2 * PANEL)
    tiles = PANEL // NB // N_ROW
    panels = inverse.reshape(2, N_ROW, tiles, NB, PANEL).transpose(0, 2, 1, 3, 4).reshape(2, PANEL, PANEL)
    current = to_global_rows(rhs)
    start = NWIN - 2 * PANEL
    solution_one = matmul(panels[1], current[start + PANEL:])
    current = jnp.concatenate([current[:start + PANEL], solution_one], axis=0)
    upper_rows = current[:start + PANEL] - matmul(upper[:start + PANEL, PANEL:], solution_one)
    current = jnp.concatenate([upper_rows, current[start + PANEL:]], axis=0)
    solution_zero = matmul(panels[0], current[start:start + PANEL])
    upper_rows = current[:start] - matmul(upper[:start, :PANEL], solution_zero)
    current = jnp.concatenate([upper_rows, solution_zero, current[start + PANEL:]], axis=0)
    return to_stored_rows(current)
```

```python
import functools

import jax
import jax.numpy as jnp
from jax import lax
from jax.experimental import pallas as pl
from jax.experimental.pallas import tpu as pltpu
from jax.sharding import PartitionSpec as P

MESH = pl.DeviceIdType.MESH
T = 256
W = 128
NY = 4
NQ = 8
NCH = 8


def kernel(fac, inv, rhs, out,
           G, PT, RB, XB, XS, B0, PA, RA, AT, AB, RH, OA,
           lsem, bsem, bss, gss, grs, dss, drs, rss, rrs, ass, ars,
           zss, zrs, oss, ors, fss, frs):
    row = lax.axis_index("row")
    col = lax.axis_index("col")
    y, zl = lax.div(row, 2), lax.rem(row, 2)
    Q, c = lax.div(col, 2), lax.rem(col, 2)
    yo, so = lax.rem(Q, NY), lax.div(Q, NY)

    def dev(y_, zl_, q_, c_):
        return (2 * y_ + zl_, 2 * q_ + c_)

    def yy(d):
        return lax.rem(y + d, NY)

    up, down, far = yy(1), yy(3), yy(2)
    home = y == yo

    def remote(src, dst, ssem, rsem, device):
        return pltpu.make_async_remote_copy(
            src_ref=src, dst_ref=dst, send_sem=ssem, recv_sem=rsem,
            device_id=device, device_id_type=MESH)

    def signal(device):
        pl.semaphore_signal(bar, inc=1, device_id=device, device_id_type=MESH)

    bar = pltpu.get_barrier_semaphore()
    for d in (1, 2, 3):
        signal(dev(yy(d), zl, Q, c))
    signal(dev(y, zl, Q, 1 - c))
    signal(dev(y, 1 - zl, Q, c))
    for d in range(1, NQ):
        signal(dev(y, zl, lax.rem(Q + d, NQ), c))
    for s in range(2):
        for d in range(NY):
            yd = yy(d)
            if d == 0:
                @pl.when(Q != y + NY * s)
                def _():
                    signal(dev(y, zl, y + NY * s, c))
            else:
                signal(dev(yd, zl, y + NY * s, c))
    pl.semaphore_wait(bar, 12 + 8 - jnp.where(home, 1, 0).astype(jnp.int32))

    def own(i):
        if i < 2:
            return inv.at[1, pl.ds(T * i, T), :]
        if i < 4:
            return fac.at[pl.ds(T * (i - 1), T), pl.ds(T, T)]
        if i < 6:
            return inv.at[0, pl.ds(T * (i - 4), T), :]
        if i == 6:
            return fac.at[pl.ds(0, T), pl.ds(T, T)]
        return fac.at[pl.ds(0, T), pl.ds(0, T)]

    def blk(i, yb):
        return G.at[i, c, yb]

    def own_up(i):
        return remote(own(i), blk(i, y), gss.at[i, 0], grs.at[i, 0], dev(up, zl, Q, c))

    def own_down(i):
        return remote(own(i), blk(i, y), gss.at[i, 1], grs.at[i, 1], dev(down, zl, Q, c))

    def relay_up(i):
        r = G.at[i, c, down, pl.ds(0, T // 2), :]
        return remote(r, r, gss.at[i, 2], grs.at[i, 2], dev(up, zl, Q, c))

    def relay_down(i):
        r = G.at[i, c, up, pl.ds(T // 2, T // 2), :]
        return remote(r, r, gss.at[i, 3], grs.at[i, 3], dev(down, zl, Q, c))

    sib = dev(y, zl, Q, 1 - c)

    def share(i, j):
        yb = (y, down, up, far)[j]
        src = own(i) if j == 0 else blk(i, yb)
        return remote(src, blk(i, yb), dss.at[i, j], drs.at[i, j], sib)

    def wait_block(i, yb, sem):
        r = blk(i, yb)
        pltpu.make_async_copy(r, r, sem).wait()

    def wait_half(i, half, sem):
        r = G.at[i, c, far, pl.ds(half * (T // 2), T // 2), :]
        pltpu.make_async_copy(r, r, sem).wait()

    def wait_share(i, j):
        yb = (y, down, up, far)[j]
        r = G.at[i, 1 - c, yb]
        pltpu.make_async_copy(r, r, drs.at[i, j]).wait()

    def send_own(i):
        own_up(i).start()
        own_down(i).start()

    def near(i):
        wait_block(i, down, grs.at[i, 0])
        relay_up(i).start()
        wait_block(i, up, grs.at[i, 1])
        relay_down(i).start()
        share(i, 1).start()
        share(i, 2).start()
        if i + 2 < NCH:
            send_own(i + 2)

    def distant(i):
        wait_half(i, 0, grs.at[i, 2])
        wait_half(i, 1, grs.at[i, 3])
        share(i, 3).start()

    def cols(y_, c_):
        return pl.ds(pl.multiple_of((c_ * NY + y_) * W, W), W)

    def rows(b):
        return pl.ds(pl.multiple_of(b * T, T), T)

    def b_dst(n):
        return XB.at[0, zl] if n == 0 else B0

    def b_move(n, d):
        b = (3 if n == 0 else 1) + so
        yd = yy(d)
        return remote(rhs.at[rows(b), cols(yd, c)], b_dst(n),
                      bss.at[n, d], bsem.at[n], dev(yd, zl, Q, c))

    def b_local(n):
        b = (3 if n == 0 else 1) + so
        return pltpu.make_async_copy(rhs.at[rows(b), cols(y, c)], b_dst(n), bsem.at[n])

    def zmove(st):
        return remote(XB.at[st, zl], XB.at[st, zl], zss.at[st], zrs.at[st],
                      dev(y, 1 - zl, Q, c))

    def zwait(st):
        r = XB.at[st, 1 - zl]
        pltpu.make_async_copy(r, r, zrs.at[st]).wait()

    def split(st, k):
        v = XB[st, k]
        hi = v.astype(jnp.bfloat16)
        lo = (v - hi.astype(jnp.float32)).astype(jnp.bfloat16)
        XS[st, k, :, pl.ds(0, W)] = hi
        XS[st, k, :, pl.ds(W, W)] = lo

    def product(i, yb, st):
        total = None
        for k in range(2):
            a = G[i, k, yb]
            hi = a.astype(jnp.bfloat16)
            lo = (a - hi.astype(jnp.float32)).astype(jnp.bfloat16)
            x = XS[st, k]
            wide = jnp.dot(hi, x, preferred_element_type=jnp.float32)
            part = wide[:, :W] + wide[:, W:] + jnp.dot(
                lo, x[:, :W], preferred_element_type=jnp.float32)
            total = part if total is None else total + part
        return total

    def scatter(ph, t):
        return remote(PT.at[ph, t], RB.at[ph, Q], rss.at[ph, t], rrs.at[ph, Q],
                      dev(y, zl, t, c))

    def tiles(i, ph, st, lo, hi):
        s = i % 2

        def step(j, carry):
            yb = lax.rem(y + 3 + j, NY)
            t = NY * s + yb
            PT[ph, t] = product(i, yb, st)

            @pl.when(t != Q)
            def _():
                scatter(ph, t).start()
            return carry

        lax.fori_loop(lo, hi, step, 0)

    def gathered(ph):
        def step(d, total):
            src = lax.rem(Q + d, NQ)
            r = RB.at[ph, src]
            pltpu.make_async_copy(r, r, rrs.at[ph, src]).wait()
            return total + RB[ph, src]
        return lax.fori_loop(1, NQ, step, PT[ph, Q])

    def o_send(n, d):
        qd = lax.rem(Q + d, NQ)
        st = 1 if n == 1 else 3
        src = XB.at[st, zl]
        dst = out.at[rows(1 + 2 * n + so), cols(y, c)]
        return src, dst, qd

    def o_start(n):
        for d in range(NQ):
            src, dst, qd = o_send(n, d)
            if d == 0:
                @pl.when(home)
                def _():
                    pltpu.make_async_copy(src, dst, ors.at[n, NY * so + y]).start()

                @pl.when(jnp.logical_not(home))
                def _():
                    remote(src, dst, oss.at[n, 0], ors.at[n, NY * so + y],
                           dev(yo, zl, Q, c)).start()
            else:
                remote(src, dst, oss.at[n, d], ors.at[n, NY * so + y],
                       dev(yo, zl, qd, c)).start()

    def o_forward(n):
        for s in range(2):
            for yb in range(NY):
                r = out.at[rows(1 + 2 * n + s), cols(yb, c)]
                pltpu.make_async_copy(r, r, ors.at[n, NY * s + yb]).wait()
        o_share(n).start()

    def halfcols(c_):
        return pl.ds(pl.multiple_of(c_ * NY * W, NY * W), NY * W)

    def o_share(n):
        r = out.at[pl.ds((1 + 2 * n) * T, 2 * T), halfcols(c)]
        return remote(r, r, fss.at[n], frs.at[n], sib)

    def o_shared(n):
        r = out.at[pl.ds((1 + 2 * n) * T, 2 * T), halfcols(1 - c)]
        pltpu.make_async_copy(r, r, frs.at[n]).wait()

    for n in range(2):
        @pl.when(home)
        def _():
            b_local(n).start()
            for d in (1, 2, 3):
                b_move(n, d).start()
        if n == 0:
            send_own(0)
            share(0, 0).start()
    locals_ = [pltpu.make_async_copy(own(i), blk(i, y), lsem.at[i]) for i in range(NCH)]
    rh_copy = pltpu.make_async_copy(rhs.at[pl.ds(0, T), :], RH, lsem.at[NCH])
    for cp in locals_:
        cp.start()
    send_own(1)
    for i in range(1, NCH):
        share(i, 0).start()
    rh_copy.start()

    r = b_dst(0)
    pltpu.make_async_copy(r, r, bsem.at[0]).wait()
    zmove(0).start()
    split(0, zl)
    for cp in locals_:
        cp.wait()
    rh_copy.wait()
    near(0)
    zwait(0)
    split(0, 1 - zl)
    wait_share(0, 0)
    wait_share(0, 1)
    wait_share(0, 2)
    tiles(0, 0, 0, 0, 3)
    distant(0)
    wait_share(0, 3)
    tiles(0, 0, 0, 3, 4)

    def second(i, ph, st):
        near(i)
        for j in range(3):
            wait_share(i, j)
        tiles(i, ph, st, 0, 3)
        distant(i)
        wait_share(i, 3)
        tiles(i, ph, st, 3, 4)

    def first(i, ph, st):
        distant(i)
        for j in range(4):
            wait_share(i, j)
        tiles(i, ph, st, 0, 4)

    def finish(ph, st, nxt):
        total = gathered(ph)
        if st == 2:
            pltpu.make_async_copy(B0, B0, bsem.at[1]).wait()
            XB[st, zl] = B0[...] - total
        else:
            XB[st, zl] = total
        zmove(st).start()
        split(st, zl)
        near(nxt)
        if st == 1:
            o_start(1)
        if st == 3:
            o_start(0)
        zwait(st)
        split(st, 1 - zl)

    second(1, 0, 0)
    finish(0, 1, 2)
    first(2, 1, 1)
    second(3, 1, 1)
    finish(1, 2, 4)
    o_forward(1)
    first(4, 2, 2)
    second(5, 2, 2)
    finish(2, 3, 6)

    def a_move(yb, h):
        return remote(PA.at[yb, pl.ds(h * (T // 2), T // 2), :], RA.at[Q],
                      ass.at[NY * h + yb], ars.at[Q], dev(y, zl, NY * h + yb, c))

    def above(lo, hi):
        def step(j, carry):
            yb = lax.rem(y + 3 + j, NY)
            PA[yb] = product(6, yb, 1) + product(7, yb, 3)
            for h in range(2):
                @pl.when(NY * h + yb != Q)
                def _():
                    a_move(yb, h).start()
            return carry
        lax.fori_loop(lo, hi, step, 0)

    distant(6)
    for j in range(4):
        wait_share(6, j)
    near(7)
    for j in range(3):
        wait_share(7, j)
    above(0, 3)
    distant(7)
    wait_share(7, 3)
    above(3, 4)
    o_forward(0)

    def a_step(d, total):
        src = lax.rem(Q + d, NQ)
        r = RA.at[src]
        pltpu.make_async_copy(r, r, ars.at[src]).wait()
        return total + RA[src]

    half = pl.ds(pl.multiple_of(so * (T // 2), T // 2), T // 2)
    AT[...] = lax.fori_loop(1, NQ, a_step, PA[yo, half, :])

    a_dst = AB.at[half, cols(y, c)]
    a_sem = ors.at[2, NY * so + y]

    @pl.when(home)
    def _():
        pltpu.make_async_copy(AT, a_dst, a_sem).start()

    @pl.when(jnp.logical_not(home))
    def _():
        remote(AT, a_dst, oss.at[2, 0], a_sem, dev(yo, zl, Q, c)).start()

    for d in range(1, NQ):
        remote(AT, a_dst, oss.at[2, d], a_sem,
               dev(yo, zl, lax.rem(Q + d, NQ), c)).start()
    for s in range(2):
        for yb in range(NY):
            r = AB.at[pl.ds(s * (T // 2), T // 2), cols(yb, c)]
            pltpu.make_async_copy(r, r, ors.at[2, NY * s + yb]).wait()
    mine = AB.at[:, halfcols(c)]
    a_share = remote(mine, mine, fss.at[2], frs.at[2], sib)
    a_share.start()
    OA[:, halfcols(c)] = RH[:, halfcols(c)] - AB[:, halfcols(c)]
    w0 = pltpu.make_async_copy(OA.at[:, halfcols(c)], out.at[pl.ds(0, T), halfcols(c)], lsem.at[0])
    w0.start()
    theirs = AB.at[:, halfcols(1 - c)]
    pltpu.make_async_copy(theirs, theirs, frs.at[2]).wait()
    OA[:, halfcols(1 - c)] = RH[:, halfcols(1 - c)] - AB[:, halfcols(1 - c)]
    w1 = pltpu.make_async_copy(OA.at[:, halfcols(1 - c)], out.at[pl.ds(0, T), halfcols(1 - c)], lsem.at[1])
    w1.start()

    o_shared(1)
    o_shared(0)
    w0.wait()
    w1.wait()
    for n in range(2):
        @pl.when(home)
        def _():
            for d in (1, 2, 3):
                b_move(n, d).wait_send()
    for i in range(NCH):
        own_up(i).wait_send()
        own_down(i).wait_send()
        relay_up(i).wait_send()
        relay_down(i).wait_send()
        for j in range(4):
            share(i, j).wait_send()
    for ph in range(3):
        def drain(d, carry):
            scatter(ph, lax.rem(Q + d, NQ)).wait_send()
            return carry
        lax.fori_loop(1, NQ, drain, 0)
    for yb in range(NY):
        for h in range(2):
            @pl.when(NY * h + yb != Q)
            def _():
                a_move(yb, h).wait_send()
    for st in range(4):
        zmove(st).wait_send()
    for n in range(2):
        src, dst, _ = o_send(n, 0)

        @pl.when(jnp.logical_not(home))
        def _():
            remote(src, dst, oss.at[n, 0], ors.at[n, 0], dev(yo, zl, Q, c)).wait_send()
        for d in range(1, NQ):
            src, dst, qd = o_send(n, d)
            remote(src, dst, oss.at[n, d], ors.at[n, 0], dev(yo, zl, qd, c)).wait_send()
        o_share(n).wait_send()

    @pl.when(jnp.logical_not(home))
    def _():
        remote(AT, a_dst, oss.at[2, 0], a_sem, dev(yo, zl, Q, c)).wait_send()
    for d in range(1, NQ):
        remote(AT, a_dst, oss.at[2, d], a_sem,
               dev(yo, zl, lax.rem(Q + d, NQ), c)).wait_send()
    a_share.wait_send()


def shards(factor, inverse, rhs):
    f32, bf16 = jnp.float32, jnp.bfloat16
    dma = pltpu.SemaphoreType.DMA
    return pl.pallas_call(
        kernel,
        out_shape=jax.ShapeDtypeStruct(rhs.shape, f32),
        in_specs=[pl.BlockSpec(memory_space=pl.ANY)] * 3,
        out_specs=pl.BlockSpec(memory_space=pl.ANY),
        scratch_shapes=[
            pltpu.VMEM((NCH, 2, NY, T, T), f32),
            pltpu.VMEM((3, NQ, T, W), f32),
            pltpu.VMEM((3, NQ, T, W), f32),
            pltpu.VMEM((4, 2, T, W), f32),
            pltpu.VMEM((4, 2, T, 2 * W), bf16),
            pltpu.VMEM((T, W), f32),
            pltpu.VMEM((NY, T, W), f32),
            pltpu.VMEM((NQ, T // 2, W), f32),
            pltpu.VMEM((T // 2, W), f32),
            pltpu.VMEM((T, NQ * W), f32),
            pltpu.VMEM((T, NQ * W), f32),
            pltpu.VMEM((T, NQ * W), f32),
            dma((NCH + 1,)),
            dma((2,)), dma((2, 4)),
            dma((NCH, 4)), dma((NCH, 4)),
            dma((NCH, 4)), dma((NCH, 4)),
            dma((3, NQ)), dma((3, NQ)),
            dma((NQ,)), dma((NQ,)),
            dma((4,)), dma((4,)),
            dma((3, NQ)), dma((3, NQ)),
            dma((3,)), dma((3,)),
        ],
        compiler_params=pltpu.CompilerParams(
            collective_id=0, has_side_effects=True, vmem_limit_bytes=56 * 2**20),
        name="panel_steps",
    )(factor, inverse, rhs)


def solution(mesh):
    return jax.shard_map(
        shards,
        mesh=mesh,
        in_specs=(P("row", "col"), P(None, "row", "col"), P("row", None)),
        out_specs=P("row", None),
        check_vma=False,
    )
```

```python
import functools

import jax
import jax.numpy as jnp
from jax import lax
from jax.experimental import pallas as pl
from jax.experimental.pallas import tpu as pltpu
from jax.sharding import PartitionSpec as P

MESH = pl.DeviceIdType.MESH
T = 256
W = 128
NY = 4
NQ = 8
NCH = 8
E = 32
WINDOW = 2


def kernel(fac, inv, rhs, out,
           G, PT, RB, XB, XS, B0, PA, RA, AB, RH, OA,
           lsem, bss, brs, gss, grs, dss, drs, rss, rrs, ass, ars,
           zss, zrs, oss, ors, ess, ers, fss, frs, yss):
    row = lax.axis_index("row")
    col = lax.axis_index("col")
    y, zl = lax.div(row, 2), lax.rem(row, 2)
    Q, c = lax.div(col, 2), lax.rem(col, 2)
    yo, so = lax.rem(Q, NY), lax.div(Q, NY)

    def dev(y_, zl_, q_, c_):
        return (2 * y_ + zl_, 2 * q_ + c_)

    def yy(d):
        return lax.rem(y + d, NY)

    def qq(d):
        return lax.rem(Q + d, NQ)

    up, down, far = yy(1), yy(3), yy(2)
    home = y == yo
    sib = dev(y, zl, Q, 1 - c)

    def remote(src, dst, ssem, rsem, device):
        return pltpu.make_async_remote_copy(
            src_ref=src, dst_ref=dst, send_sem=ssem, recv_sem=rsem,
            device_id=device, device_id_type=MESH)

    def arrived(r, sem):
        pltpu.make_async_copy(r, r, sem).wait()

    def signal(device):
        pl.semaphore_signal(bar, inc=1, device_id=device, device_id_type=MESH)

    bar = pltpu.get_barrier_semaphore()
    for e in range(1, NY * NQ):
        signal(dev(yy(e // NQ), zl, qq(e % NQ), c))
    signal(sib)
    signal(dev(y, 1 - zl, Q, c))
    pl.semaphore_wait(bar, NY * NQ + 1)

    def own(i):
        if i < 2:
            return inv.at[1, :, i]
        if i < 4:
            return fac.at[pl.ds(1, 2), i - 2, :, pl.ds(T, T)]
        if i < 6:
            return inv.at[0, :, i - 4]
        if i == 6:
            return fac.at[0, :, :, pl.ds(T, T)]
        return fac.at[0, :, :, pl.ds(0, T)]

    def blk(i, yb):
        return G.at[i, c, yb]

    def own_up(i):
        return remote(own(i), blk(i, y), gss.at[i, 0], grs.at[i, 0], dev(up, zl, Q, c))

    def own_down(i):
        return remote(own(i), blk(i, y), gss.at[i, 1], grs.at[i, 1], dev(down, zl, Q, c))

    def relay_up(i):
        r = G.at[i, c, down, 0]
        return remote(r, r, gss.at[i, 2], grs.at[i, 2], dev(up, zl, Q, c))

    def relay_down(i):
        r = G.at[i, c, up, 1]
        return remote(r, r, gss.at[i, 3], grs.at[i, 3], dev(down, zl, Q, c))

    def share(i, j):
        yb = (y, down, up, far)[j]
        src = own(i) if j == 0 else blk(i, yb)
        return remote(src, blk(i, yb), dss.at[i, j], drs.at[i, j], sib)

    def wait_share(i, j):
        yb = (y, down, up, far)[j]
        arrived(G.at[i, 1 - c, yb], drs.at[i, j])

    def send_own(i):
        own_up(i).start()
        own_down(i).start()

    def near(i):
        arrived(blk(i, down), grs.at[i, 0])
        relay_up(i).start()
        arrived(blk(i, up), grs.at[i, 1])
        relay_down(i).start()
        share(i, 1).start()
        share(i, 2).start()
        if i + WINDOW < NCH:
            send_own(i + WINDOW)

    def distant(i):
        arrived(G.at[i, c, far, 0], grs.at[i, 2])
        arrived(G.at[i, c, far, 1], grs.at[i, 3])
        share(i, 3).start()

    def cols(y_, c_):
        return pl.ds(pl.multiple_of((c_ * NY + y_) * W, W), W)

    def halfcols(c_):
        return pl.ds(pl.multiple_of(c_ * NY * W, NY * W), NY * W)

    def piece(q_):
        return pl.ds(pl.multiple_of(q_ * E, E), E)

    def b_dst(n, q_):
        return XB.at[0, zl, piece(q_)] if n == 0 else B0.at[piece(q_)]

    def b_each(n, do):
        for s in range(2):
            b = (3 if n == 0 else 1) + s
            qd = y + NY * s
            for d in range(NY):
                yd = yy(d)
                src = rhs.at[b, piece(Q), cols(yd, c)]
                dst = b_dst(n, Q)

                def far_copy():
                    return remote(src, dst, bss.at[n, s, d], brs.at[n, Q], dev(yd, zl, qd, c))
                if d == 0:
                    if do == "start":
                        @pl.when(qd == Q)
                        def _():
                            pltpu.make_async_copy(src, dst, brs.at[n, Q]).start()

                    @pl.when(qd != Q)
                    def _():
                        far_copy().start() if do == "start" else far_copy().wait_send()
                else:
                    far_copy().start() if do == "start" else far_copy().wait_send()

    def b_wait(n):
        for q_ in range(NQ):
            arrived(b_dst(n, q_), brs.at[n, q_])

    def halfrows(h):
        return pl.ds(h * (T // 2), T // 2)

    def zmove(st, h):
        r = XB.at[st, zl, halfrows(h)]
        return remote(r, r, zss.at[st, h], zrs.at[st, h], dev(y, 1 - zl, Q, c))

    def split(st, k, h):
        v = XB[st, k, halfrows(h), :]
        hi = v.astype(jnp.bfloat16)
        lo = (v - hi.astype(jnp.float32)).astype(jnp.bfloat16)
        XS[st, k, halfrows(h), pl.ds(0, W)] = hi
        XS[st, k, halfrows(h), pl.ds(W, W)] = lo

    def zdone(st):
        for h in range(2):
            arrived(XB.at[st, 1 - zl, halfrows(h)], zrs.at[st, h])
            split(st, 1 - zl, h)

    def product(i, yb, st):
        total = None
        for k in range(2):
            a = G[i, k, yb].reshape(T, T)
            hi = a.astype(jnp.bfloat16)
            lo = (a - hi.astype(jnp.float32)).astype(jnp.bfloat16)
            x = XS[st, k]
            wide = jnp.dot(hi, x, preferred_element_type=jnp.float32)
            part = wide[:, :W] + wide[:, W:] + jnp.dot(
                lo, x[:, :W], preferred_element_type=jnp.float32)
            total = part if total is None else total + part
        return total

    def scatter(ph, t, h):
        return remote(PT.at[ph, t, h], RB.at[ph, Q, h], rss.at[ph, t, h], rrs.at[ph, Q, h],
                      dev(y, zl, t, c))

    def tiles(i, ph, st, lo, hi):
        h = i % 2

        def step(j, carry):
            yb = lax.rem(y + 3 + j, NY)
            total = product(i, yb, st)
            for s in range(2):
                t = NY * s + yb
                PT[ph, t, h] = total[s * (T // 2):(s + 1) * (T // 2)]

                @pl.when(t != Q)
                def _():
                    scatter(ph, t, h).start()
            return carry

        lax.fori_loop(lo, hi, step, 0)

    def gathered(ph, h):
        def step(d, total):
            src = qq(d)
            arrived(RB.at[ph, src, h], rrs.at[ph, src, h])
            return total + RB[ph, src, h]
        return lax.fori_loop(1, NQ, step, PT[ph, Q, h])

    def o_each(n, do):
        st = 1 if n == 1 else 3
        for d in range(NQ):
            qd = qq(d)
            src = XB.at[st, zl, piece(qd)]
            dst = out.at[1 + 2 * n + so, piece(qd), cols(y, c)]
            sem = ors.at[n, NY * so + y]

            def far_copy():
                return remote(src, dst, oss.at[n, d], sem, dev(yo, zl, qd, c))
            if d == 0:
                if do == "start":
                    @pl.when(home)
                    def _():
                        pltpu.make_async_copy(src, dst, sem).start()

                @pl.when(jnp.logical_not(home))
                def _():
                    far_copy().start() if do == "start" else far_copy().wait_send()
            else:
                far_copy().start() if do == "start" else far_copy().wait_send()

    def o_spread(n, s, d):
        r = out.at[1 + 2 * n + s, piece(Q), halfcols(c)]
        return remote(r, r, ess.at[n, s, d], ers.at[n, s, Q], dev(y, zl, qq(d), c))

    def o_turn(n, s):
        for yb in range(NY):
            arrived(out.at[1 + 2 * n + s, piece(Q), cols(yb, c)], ors.at[n, NY * s + yb])
        for d in range(1, NQ):
            o_spread(n, s, d).start()

    def o_share(n):
        r = out.at[pl.ds(1 + 2 * n, 2), :, halfcols(c)]
        return remote(r, r, fss.at[n], frs.at[n], sib)

    def o_forward(n):
        for d in range(1, NQ):
            for s in range(2):
                arrived(out.at[1 + 2 * n + s, piece(qq(d)), halfcols(c)], ers.at[n, s, qq(d)])
        o_share(n).start()

    send_own(0)
    b_each(0, "start")
    share(0, 0).start()
    locals_ = [pltpu.make_async_copy(own(i), blk(i, y), lsem.at[i]) for i in range(NCH)]
    rh_copy = pltpu.make_async_copy(rhs.at[0], RH, lsem.at[NCH])
    for cp in locals_:
        cp.start()
    rh_copy.start()
    own_up(0).wait_send()
    own_down(0).wait_send()
    send_own(1)
    share(1, 0).start()
    b_wait(0)
    for h in range(2):
        zmove(0, h).start()
        split(0, zl, h)
    near(0)
    for cp in locals_:
        cp.wait()
    rh_copy.wait()
    for i in range(2, NCH):
        share(i, 0).start()
    zdone(0)
    for j in range(3):
        wait_share(0, j)
    tiles(0, 0, 0, 0, 3)
    near(1)
    distant(0)
    wait_share(0, 3)
    tiles(0, 0, 0, 3, 4)
    for j in range(3):
        wait_share(1, j)
    tiles(1, 0, 0, 0, 3)
    distant(1)
    wait_share(1, 3)
    tiles(1, 0, 0, 3, 4)
    b_each(1, "start")

    def sent(ph):
        def step(d, carry):
            scatter(ph, qq(d), 0).wait_send()
            scatter(ph, qq(d), 1).wait_send()
            return carry
        lax.fori_loop(1, NQ, step, 0)

    def finish(ph, st, h):
        total = gathered(ph, h)
        if st == 2:
            XB[st, zl, halfrows(h), :] = B0[halfrows(h), :] - total
        else:
            XB[st, zl, halfrows(h), :] = total
        zmove(st, h).start()
        split(st, zl, h)

    def whole(i, ph, st):
        for j in range(4):
            wait_share(i, j)
        tiles(i, ph, st, 0, 4)

    near(2)
    finish(0, 1, 0)
    finish(0, 1, 1)
    o_each(1, "start")
    distant(2)
    zdone(1)
    whole(2, 1, 1)
    near(3)
    distant(3)
    whole(3, 1, 1)
    near(4)
    b_wait(1)
    sent(1)
    o_turn(1, 0)
    finish(1, 2, 0)
    distant(4)
    near(5)
    finish(1, 2, 1)
    o_turn(1, 1)
    zdone(2)
    whole(4, 2, 2)
    distant(5)
    whole(5, 2, 2)
    near(6)
    distant(6)
    near(7)
    o_forward(1)
    for j in range(4):
        wait_share(6, j)

    def above_one(j, carry):
        yb = lax.rem(y + 3 + j, NY)
        PA[yb] = product(6, yb, 1)
        return carry
    lax.fori_loop(0, NY, above_one, 0)
    finish(2, 3, 0)
    finish(2, 3, 1)
    o_each(0, "start")
    distant(7)
    zdone(3)
    for j in range(4):
        wait_share(7, j)

    def above_two(j, carry):
        yb = lax.rem(y + 3 + j, NY)
        PA[yb] = PA[yb] + product(7, yb, 3)
        return carry
    lax.fori_loop(0, NY, above_two, 0)

    def a_each(do):
        for e in range(NY * NQ):
            yd, qd = yy(e // NQ), qq(e % NQ)
            src, dst = PA.at[yd, piece(qd)], RA.at[y, Q]
            if e == 0:
                if do == "start":
                    pltpu.make_async_copy(src, dst, ars.at[y]).start()
            else:
                far_copy = remote(src, dst, ass.at[e], ars.at[y], dev(yd, zl, qd, c))
                far_copy.start() if do == "start" else far_copy.wait_send()

    a_each("start")
    a_each("end")
    o_turn(0, 0)
    for yb in range(NY):
        arrived(RA.at[yb], ars.at[yb])
        total = RA[yb, 0]
        for q_ in range(1, NQ):
            total = total + RA[yb, q_]
        AB[piece(Q), cols(yb, c)] = total

    def a_part(q_, c_):
        return AB.at[piece(q_), halfcols(c_)]

    def a_spread(d):
        return remote(a_part(Q, c), a_part(Q, c), ess.at[2, 0, d], ers.at[2, 0, Q],
                      dev(y, zl, qq(d), c))

    def a_share(d):
        r = a_part(qq(d), c)
        return remote(r, r, yss.at[d], frs.at[2 + qq(d)], sib)

    for d in range(1, NQ):
        a_spread(d).start()
    a_share(0).start()
    o_turn(0, 1)
    for d in range(1, NQ):
        arrived(a_part(qq(d), c), ers.at[2, 0, qq(d)])
        a_share(d).start()
    OA[:, halfcols(c)] = RH[:, halfcols(c)] - AB[:, halfcols(c)]
    w0 = pltpu.make_async_copy(OA.at[:, halfcols(c)], out.at[0, :, halfcols(c)], lsem.at[0])
    w0.start()
    for d in range(NQ):
        arrived(a_part(qq(d), 1 - c), frs.at[2 + qq(d)])
    OA[:, halfcols(1 - c)] = RH[:, halfcols(1 - c)] - AB[:, halfcols(1 - c)]
    w1 = pltpu.make_async_copy(OA.at[:, halfcols(1 - c)], out.at[0, :, halfcols(1 - c)], lsem.at[1])
    w1.start()
    o_forward(0)

    for n in range(2):
        arrived(out.at[pl.ds(1 + 2 * n, 2), :, halfcols(1 - c)], frs.at[n])
    w0.wait()
    w1.wait()
    for i in range(NCH):
        if i:
            own_up(i).wait_send()
            own_down(i).wait_send()
        relay_up(i).wait_send()
        relay_down(i).wait_send()
        for j in range(4):
            share(i, j).wait_send()
    sent(0)
    sent(2)
    for st in range(4):
        zmove(st, 0).wait_send()
        zmove(st, 1).wait_send()
    for n in range(2):
        b_each(n, "end")
        o_each(n, "end")
        for d in range(1, NQ):
            o_spread(n, 0, d).wait_send()
            o_spread(n, 1, d).wait_send()
        o_share(n).wait_send()
    for d in range(1, NQ):
        a_spread(d).wait_send()
    for d in range(NQ):
        a_share(d).wait_send()


def shards(factor, inverse, rhs):
    f32, bf16 = jnp.float32, jnp.bfloat16
    dma = pltpu.SemaphoreType.DMA
    solved = pl.pallas_call(
        kernel,
        out_shape=jax.ShapeDtypeStruct((5, T, NQ * W), f32),
        in_specs=[pl.BlockSpec(memory_space=pl.ANY)] * 3,
        out_specs=pl.BlockSpec(memory_space=pl.ANY),
        scratch_shapes=[
            pltpu.VMEM((NCH, 2, NY, 2, T // 2, T), f32),
            pltpu.VMEM((3, NQ, 2, T // 2, W), f32),
            pltpu.VMEM((3, NQ, 2, T // 2, W), f32),
            pltpu.VMEM((4, 2, T, W), f32),
            pltpu.VMEM((4, 2, T, 2 * W), bf16),
            pltpu.VMEM((T, W), f32),
            pltpu.VMEM((NY, T, W), f32),
            pltpu.VMEM((NY, NQ, E, W), f32),
            pltpu.VMEM((T, NQ * W), f32),
            pltpu.VMEM((T, NQ * W), f32),
            pltpu.VMEM((T, NQ * W), f32),
            dma((NCH + 1,)),
            dma((2, 2, NY)), dma((2, NQ)),
            dma((NCH, 4)), dma((NCH, 4)),
            dma((NCH, 4)), dma((NCH, 4)),
            dma((3, NQ, 2)), dma((3, NQ, 2)),
            dma((NY * NQ,)), dma((NY,)),
            dma((4, 2)), dma((4, 2)),
            dma((2, NQ)), dma((2, NQ)),
            dma((3, 2, NQ)), dma((3, 2, NQ)),
            dma((2,)), dma((2 + NQ,)),
            dma((NQ,)),
        ],
        compiler_params=pltpu.CompilerParams(
            collective_id=0, has_side_effects=True, vmem_limit_bytes=56 * 2**20),
        name="panel_steps",
    )(factor.reshape(5, 2, T // 2, 2 * T), inverse.reshape(2, 2, 2, T // 2, T),
      rhs.reshape(5, T, NQ * W))
    return solved.reshape(rhs.shape)


def solution(mesh):
    return jax.shard_map(
        shards,
        mesh=mesh,
        in_specs=(P("row", "col"), P(None, "row", "col"), P("row", None)),
        out_specs=P("row", None),
        check_vma=False,
    )
```

```python
import functools

import jax
import jax.numpy as jnp
from jax import lax
from jax.experimental import pallas as pl
from jax.experimental.pallas import tpu as pltpu
from jax.sharding import PartitionSpec as P

MESH = pl.DeviceIdType.MESH
T = 256
W = 128
NY = 4
NQ = 8
NCH = 8
E = 32
WINDOW = 2


def kernel(fac, inv, rhs, out,
           G, PT, RB, XB, XS, B0, PA, RA, AB, RH,
           lsem, bss, brs, gss, grs, dss, drs, rss, rrs, ass, ars,
           zss, zrs, oss, ors, ess, ers, fss, frs, yss, ars2):
    row = lax.axis_index("row")
    col = lax.axis_index("col")
    y, zl = lax.div(row, 2), lax.rem(row, 2)
    Q, c = lax.div(col, 2), lax.rem(col, 2)
    yo, so = lax.rem(Q, NY), lax.div(Q, NY)

    def dev(y_, zl_, q_, c_):
        return (2 * y_ + zl_, 2 * q_ + c_)

    def yy(d):
        return lax.rem(y + d, NY)

    def qq(d):
        return lax.rem(Q + d, NQ)

    up, down, far = yy(1), yy(3), yy(2)
    home = y == yo
    sib = dev(y, zl, Q, 1 - c)

    def remote(src, dst, ssem, rsem, device):
        return pltpu.make_async_remote_copy(
            src_ref=src, dst_ref=dst, send_sem=ssem, recv_sem=rsem,
            device_id=device, device_id_type=MESH)

    def arrived(r, sem):
        pltpu.make_async_copy(r, r, sem).wait()

    def signal(device):
        pl.semaphore_signal(bar, inc=1, device_id=device, device_id_type=MESH)

    bar = pltpu.get_barrier_semaphore()
    for e in range(1, NY * NQ):
        signal(dev(yy(e // NQ), zl, qq(e % NQ), c))
    signal(sib)
    signal(dev(y, 1 - zl, Q, c))
    pl.semaphore_wait(bar, NY * NQ + 1)

    def own(i):
        if i < 2:
            return inv.at[1, :, i]
        if i < 4:
            return fac.at[pl.ds(1, 2), i - 2, :, pl.ds(T, T)]
        if i < 6:
            return inv.at[0, :, i - 4]
        if i == 6:
            return fac.at[0, :, :, pl.ds(T, T)]
        return fac.at[0, :, :, pl.ds(0, T)]

    def blk(i, yb):
        return G.at[i, c, yb]

    def own_up(i):
        return remote(own(i), blk(i, y), gss.at[i, 0], grs.at[i, 0], dev(up, zl, Q, c))

    def own_down(i):
        return remote(own(i), blk(i, y), gss.at[i, 1], grs.at[i, 1], dev(down, zl, Q, c))

    def relay_up(i):
        r = G.at[i, c, down, 0]
        return remote(r, r, gss.at[i, 2], grs.at[i, 2], dev(up, zl, Q, c))

    def relay_down(i):
        r = G.at[i, c, up, 1]
        return remote(r, r, gss.at[i, 3], grs.at[i, 3], dev(down, zl, Q, c))

    def share(i, j):
        yb = (y, down, up, far)[j]
        src = own(i) if j == 0 else blk(i, yb)
        return remote(src, blk(i, yb), dss.at[i, j], drs.at[i, j], sib)

    def wait_share(i, j):
        yb = (y, down, up, far)[j]
        arrived(G.at[i, 1 - c, yb], drs.at[i, j])

    def send_own(i):
        own_up(i).start()
        own_down(i).start()

    def near(i):
        arrived(blk(i, down), grs.at[i, 0])
        relay_up(i).start()
        arrived(blk(i, up), grs.at[i, 1])
        relay_down(i).start()
        share(i, 1).start()
        share(i, 2).start()
        if i + WINDOW < NCH:
            send_own(i + WINDOW)

    def distant(i):
        arrived(G.at[i, c, far, 0], grs.at[i, 2])
        arrived(G.at[i, c, far, 1], grs.at[i, 3])
        share(i, 3).start()

    def cols(y_, c_):
        return pl.ds(pl.multiple_of((c_ * NY + y_) * W, W), W)

    def halfcols(c_):
        return pl.ds(pl.multiple_of(c_ * NY * W, NY * W), NY * W)

    def piece(q_):
        return pl.ds(pl.multiple_of(q_ * E, E), E)

    def b_dst(n, q_):
        return XB.at[0, zl, piece(q_)] if n == 0 else B0.at[piece(q_)]

    def b_each(n, do):
        for s in range(2):
            b = (3 if n == 0 else 1) + s
            qd = y + NY * s
            for d in range(NY):
                yd = yy(d)
                src = rhs.at[b, piece(Q), cols(yd, c)]
                dst = b_dst(n, Q)

                def far_copy():
                    return remote(src, dst, bss.at[n, s, d], brs.at[n, Q], dev(yd, zl, qd, c))
                if d == 0:
                    if do == "start":
                        @pl.when(qd == Q)
                        def _():
                            pltpu.make_async_copy(src, dst, brs.at[n, Q]).start()

                    @pl.when(qd != Q)
                    def _():
                        far_copy().start() if do == "start" else far_copy().wait_send()
                else:
                    far_copy().start() if do == "start" else far_copy().wait_send()

    def b_wait(n):
        for q_ in range(NQ):
            arrived(b_dst(n, q_), brs.at[n, q_])

    def halfrows(h):
        return pl.ds(h * (T // 2), T // 2)

    def zmove(st, h):
        r = XB.at[st, zl, halfrows(h)]
        return remote(r, r, zss.at[st, h], zrs.at[st, h], dev(y, 1 - zl, Q, c))

    def split(st, k, h):
        v = XB[st, k, halfrows(h), :]
        hi = v.astype(jnp.bfloat16)
        lo = (v - hi.astype(jnp.float32)).astype(jnp.bfloat16)
        XS[st, k, halfrows(h), pl.ds(0, W)] = hi
        XS[st, k, halfrows(h), pl.ds(W, W)] = lo

    def zdone(st):
        for h in range(2):
            arrived(XB.at[st, 1 - zl, halfrows(h)], zrs.at[st, h])
            split(st, 1 - zl, h)

    def product(i, yb, st):
        total = None
        for k in range(2):
            a = G[i, k, yb].reshape(T, T)
            hi = a.astype(jnp.bfloat16)
            lo = (a - hi.astype(jnp.float32)).astype(jnp.bfloat16)
            x = XS[st, k]
            wide = jnp.dot(hi, x, preferred_element_type=jnp.float32)
            part = wide[:, :W] + wide[:, W:] + jnp.dot(
                lo, x[:, :W], preferred_element_type=jnp.float32)
            total = part if total is None else total + part
        return total

    def scatter(ph, t, h):
        return remote(PT.at[ph, t, h], RB.at[ph, Q, h], rss.at[ph, t, h], rrs.at[ph, Q, h],
                      dev(y, zl, t, c))

    def tiles(i, ph, st, lo, hi):
        h = i % 2

        def step(j, carry):
            yb = lax.rem(y + 3 + j, NY)
            total = product(i, yb, st)
            for s in range(2):
                t = NY * s + yb
                PT[ph, t, h] = total[s * (T // 2):(s + 1) * (T // 2)]

                @pl.when(t != Q)
                def _():
                    scatter(ph, t, h).start()
            return carry

        lax.fori_loop(lo, hi, step, 0)

    def gathered(ph, h):
        def step(d, total):
            src = qq(d)
            arrived(RB.at[ph, src, h], rrs.at[ph, src, h])
            return total + RB[ph, src, h]
        return lax.fori_loop(1, NQ, step, PT[ph, Q, h])

    def o_each(n, do):
        st = 1 if n == 1 else 3
        for d in range(NQ):
            qd = qq(d)
            src = XB.at[st, zl, piece(qd)]
            dst = out.at[1 + 2 * n + so, piece(qd), cols(y, c)]
            sem = ors.at[n, NY * so + y]

            def far_copy():
                return remote(src, dst, oss.at[n, d], sem, dev(yo, zl, qd, c))
            if d == 0:
                if do == "start":
                    @pl.when(home)
                    def _():
                        pltpu.make_async_copy(src, dst, sem).start()

                @pl.when(jnp.logical_not(home))
                def _():
                    far_copy().start() if do == "start" else far_copy().wait_send()
            else:
                far_copy().start() if do == "start" else far_copy().wait_send()

    def o_spread(n, s, d):
        r = out.at[1 + 2 * n + s, piece(Q), halfcols(c)]
        return remote(r, r, ess.at[n, s, d], ers.at[n, s, Q], dev(y, zl, qq(d), c))

    def o_turn(n, s):
        for yb in range(NY):
            arrived(out.at[1 + 2 * n + s, piece(Q), cols(yb, c)], ors.at[n, NY * s + yb])
        for d in range(1, NQ):
            o_spread(n, s, d).start()

    def o_share(n, s):
        r = out.at[1 + 2 * n + s, :, halfcols(c)]
        return remote(r, r, fss.at[n, s], frs.at[n, s], sib)

    def o_forward(n, s):
        for d in range(1, NQ):
            arrived(out.at[1 + 2 * n + s, piece(qq(d)), halfcols(c)], ers.at[n, s, qq(d)])
        o_share(n, s).start()

    send_own(0)
    b_each(0, "start")
    share(0, 0).start()
    locals_ = [pltpu.make_async_copy(own(i), blk(i, y), lsem.at[i]) for i in range(NCH)]
    rh_copy = pltpu.make_async_copy(rhs.at[0], RH, lsem.at[NCH])
    for cp in locals_:
        cp.start()
    rh_copy.start()
    own_up(0).wait_send()
    own_down(0).wait_send()
    send_own(1)
    share(1, 0).start()
    b_wait(0)
    for h in range(2):
        zmove(0, h).start()
        split(0, zl, h)
    near(0)
    for cp in locals_:
        cp.wait()
    rh_copy.wait()
    for i in range(2, NCH):
        share(i, 0).start()
    zdone(0)
    for j in range(3):
        wait_share(0, j)
    tiles(0, 0, 0, 0, 3)
    near(1)
    distant(0)
    wait_share(0, 3)
    tiles(0, 0, 0, 3, 4)
    for j in range(3):
        wait_share(1, j)
    tiles(1, 0, 0, 0, 3)
    distant(1)
    wait_share(1, 3)
    tiles(1, 0, 0, 3, 4)
    b_each(1, "start")

    def sent(ph):
        def step(d, carry):
            scatter(ph, qq(d), 0).wait_send()
            scatter(ph, qq(d), 1).wait_send()
            return carry
        lax.fori_loop(1, NQ, step, 0)

    def finish(ph, st, h):
        total = gathered(ph, h)
        if st == 2:
            XB[st, zl, halfrows(h), :] = B0[halfrows(h), :] - total
        else:
            XB[st, zl, halfrows(h), :] = total
        zmove(st, h).start()
        split(st, zl, h)

    def whole(i, ph, st):
        for j in range(4):
            wait_share(i, j)
        tiles(i, ph, st, 0, 4)

    near(2)
    finish(0, 1, 0)
    finish(0, 1, 1)
    o_each(1, "start")
    distant(2)
    zdone(1)
    whole(2, 1, 1)
    near(3)
    distant(3)
    whole(3, 1, 1)
    near(4)
    b_wait(1)
    sent(1)
    o_turn(1, 0)
    finish(1, 2, 0)
    distant(4)
    near(5)
    finish(1, 2, 1)
    o_turn(1, 1)
    zdone(2)
    whole(4, 2, 2)
    distant(5)
    whole(5, 2, 2)
    near(6)
    distant(6)
    near(7)
    o_forward(1, 0)
    o_forward(1, 1)
    for j in range(4):
        wait_share(6, j)

    def above_one(j, carry):
        yb = lax.rem(y + 3 + j, NY)
        PA[yb] = product(6, yb, 1)
        return carry
    lax.fori_loop(0, NY, above_one, 0)
    finish(2, 3, 0)
    finish(2, 3, 1)
    o_each(0, "start")
    distant(7)
    zdone(3)
    for j in range(4):
        wait_share(7, j)

    def above_two(j, carry):
        yb = lax.rem(y + 3 + j, NY)
        PA[yb] = PA[yb] + product(7, yb, 3)
        return carry
    lax.fori_loop(0, NY, above_two, 0)

    def a_each(do):
        for e in range(NY * NQ):
            yd, qd = yy(e // NQ), qq(e % NQ)
            src, dst = PA.at[yd, piece(qd)], RA.at[y, Q]
            if e == 0:
                if do == "start":
                    pltpu.make_async_copy(src, dst, ars.at[y]).start()
            else:
                far_copy = remote(src, dst, ass.at[e], ars.at[y], dev(yd, zl, qd, c))
                far_copy.start() if do == "start" else far_copy.wait_send()

    a_each("start")
    a_each("end")
    o_turn(0, 0)
    for yb in range(NY):
        arrived(RA.at[yb], ars.at[yb])
        total = RA[yb, 0]
        for q_ in range(1, NQ):
            total = total + RA[yb, q_]
        AB[piece(Q), cols(yb, c)] = total

    def a_part(q_, c_):
        return AB.at[piece(q_), halfcols(c_)]

    def a_spread(d):
        return remote(a_part(Q, c), a_part(Q, c), ess.at[2, 0, d], ers.at[2, 0, Q],
                      dev(y, zl, qq(d), c))

    def a_share(d):
        r = a_part(qq(d), c)
        return remote(r, r, yss.at[d], ars2.at[qq(d)], sib)

    for d in range(1, NQ):
        a_spread(d).start()
    a_share(0).start()
    o_turn(0, 1)
    o_forward(0, 0)
    for d in range(1, NQ):
        arrived(a_part(qq(d), c), ers.at[2, 0, qq(d)])
        a_share(d).start()
    out[0, :, halfcols(c)] = RH[:, halfcols(c)] - AB[:, halfcols(c)]
    o_forward(0, 1)
    for d in range(NQ):
        arrived(a_part(qq(d), 1 - c), ars2.at[qq(d)])
    out[0, :, halfcols(1 - c)] = RH[:, halfcols(1 - c)] - AB[:, halfcols(1 - c)]

    for n in range(2):
        for s in range(2):
            arrived(out.at[1 + 2 * n + s, :, halfcols(1 - c)], frs.at[n, s])
    for i in range(NCH):
        if i:
            own_up(i).wait_send()
            own_down(i).wait_send()
        relay_up(i).wait_send()
        relay_down(i).wait_send()
        for j in range(4):
            share(i, j).wait_send()
    sent(0)
    sent(2)
    for st in range(4):
        zmove(st, 0).wait_send()
        zmove(st, 1).wait_send()
    for n in range(2):
        b_each(n, "end")
        o_each(n, "end")
        for d in range(1, NQ):
            o_spread(n, 0, d).wait_send()
            o_spread(n, 1, d).wait_send()
        for s in range(2):
            o_share(n, s).wait_send()
    for d in range(1, NQ):
        a_spread(d).wait_send()
    for d in range(NQ):
        a_share(d).wait_send()


def shards(factor, inverse, rhs):
    f32, bf16 = jnp.float32, jnp.bfloat16
    dma = pltpu.SemaphoreType.DMA
    solved = pl.pallas_call(
        kernel,
        out_shape=pltpu.VMEM((5, T, NQ * W), f32),
        in_specs=[pl.BlockSpec(memory_space=pltpu.HBM)] * 3,
        out_specs=pl.BlockSpec(memory_space=pltpu.VMEM),
        scratch_shapes=[
            pltpu.VMEM((NCH, 2, NY, 2, T // 2, T), f32),
            pltpu.VMEM((3, NQ, 2, T // 2, W), f32),
            pltpu.VMEM((3, NQ, 2, T // 2, W), f32),
            pltpu.VMEM((4, 2, T, W), f32),
            pltpu.VMEM((4, 2, T, 2 * W), bf16),
            pltpu.VMEM((T, W), f32),
            pltpu.VMEM((NY, T, W), f32),
            pltpu.VMEM((NY, NQ, E, W), f32),
            pltpu.VMEM((T, NQ * W), f32),
            pltpu.VMEM((T, NQ * W), f32),
            dma((NCH + 1,)),
            dma((2, 2, NY)), dma((2, NQ)),
            dma((NCH, 4)), dma((NCH, 4)),
            dma((NCH, 4)), dma((NCH, 4)),
            dma((3, NQ, 2)), dma((3, NQ, 2)),
            dma((NY * NQ,)), dma((NY,)),
            dma((4, 2)), dma((4, 2)),
            dma((2, NQ)), dma((2, NQ)),
            dma((3, 2, NQ)), dma((3, 2, NQ)),
            dma((2, 2)), dma((2, 2)),
            dma((NQ,)), dma((NQ,)),
        ],
        compiler_params=pltpu.CompilerParams(
            collective_id=0, has_side_effects=True, vmem_limit_bytes=56 * 2**20),
        name="panel_steps",
    )(factor.reshape(5, 2, T // 2, 2 * T), inverse.reshape(2, 2, 2, T // 2, T),
      rhs.reshape(5, T, NQ * W))
    return solved.reshape(rhs.shape)


def solution(mesh):
    return jax.shard_map(
        shards,
        mesh=mesh,
        in_specs=(P("row", "col"), P(None, "row", "col"), P("row", None)),
        out_specs=P("row", None),
        check_vma=False,
    )
```

```python
import functools

import jax
import jax.numpy as jnp
from jax import lax
from jax.experimental import pallas as pl
from jax.experimental.pallas import tpu as pltpu
from jax.sharding import PartitionSpec as P

MESH = pl.DeviceIdType.MESH
T = 256
W = 128
NY = 4
NQ = 8
NCH = 8
E = 32
WINDOW = 2


def kernel(fac, inv, rhs, out,
           G, PT, RB, XB, XS, B0, PA, RA, AB, RH,
           lsem, bss, brs, gss, grs, dss, drs, rss, rrs, ass, ars,
           zss, zrs, oss, ors, ess, ers, fss, frs, yss, ars2):
    row = lax.axis_index("row")
    col = lax.axis_index("col")
    y, zl = lax.div(row, 2), lax.rem(row, 2)
    Q, c = lax.div(col, 2), lax.rem(col, 2)
    yo, so = lax.rem(Q, NY), lax.div(Q, NY)

    def dev(y_, zl_, q_, c_):
        return (2 * y_ + zl_, 2 * q_ + c_)

    def yy(d):
        return lax.rem(y + d, NY)

    def qq(d):
        return lax.rem(Q + d, NQ)

    up, down, far = yy(1), yy(3), yy(2)
    home = y == yo
    sib = dev(y, zl, Q, 1 - c)

    def remote(src, dst, ssem, rsem, device):
        return pltpu.make_async_remote_copy(
            src_ref=src, dst_ref=dst, send_sem=ssem, recv_sem=rsem,
            device_id=device, device_id_type=MESH)

    def arrived(r, sem):
        pltpu.make_async_copy(r, r, sem).wait()

    def signal(device):
        pl.semaphore_signal(bar, inc=1, device_id=device, device_id_type=MESH)

    bar = pltpu.get_barrier_semaphore()
    for e in range(1, NY * NQ):
        signal(dev(yy(e // NQ), zl, qq(e % NQ), c))
    signal(sib)
    signal(dev(y, 1 - zl, Q, c))
    pl.semaphore_wait(bar, NY * NQ + 1)

    def own(i):
        if i < 2:
            return inv.at[1, :, i]
        if i < 4:
            return fac.at[pl.ds(1, 2), i - 2, :, pl.ds(T, T)]
        if i < 6:
            return inv.at[0, :, i - 4]
        if i == 6:
            return fac.at[0, :, :, pl.ds(T, T)]
        return fac.at[0, :, :, pl.ds(0, T)]

    def blk(i, yb):
        return G.at[i, c, yb]

    def own_up(i):
        return remote(own(i), blk(i, y), gss.at[i, 0], grs.at[i, 0], dev(up, zl, Q, c))

    def own_down(i):
        return remote(own(i), blk(i, y), gss.at[i, 1], grs.at[i, 1], dev(down, zl, Q, c))

    def relay_up(i):
        r = G.at[i, c, down, 0]
        return remote(r, r, gss.at[i, 2], grs.at[i, 2], dev(up, zl, Q, c))

    def relay_down(i):
        r = G.at[i, c, up, 1]
        return remote(r, r, gss.at[i, 3], grs.at[i, 3], dev(down, zl, Q, c))

    def share(i, j):
        yb = (y, down, up, far)[j]
        src = own(i) if j == 0 else blk(i, yb)
        return remote(src, blk(i, yb), dss.at[i, j], drs.at[i, j], sib)

    def wait_share(i, j):
        yb = (y, down, up, far)[j]
        arrived(G.at[i, 1 - c, yb], drs.at[i, j])

    def send_own(i):
        own_up(i).start()
        own_down(i).start()

    def near(i):
        arrived(blk(i, down), grs.at[i, 0])
        relay_up(i).start()
        arrived(blk(i, up), grs.at[i, 1])
        relay_down(i).start()
        share(i, 1).start()
        share(i, 2).start()
        if i + WINDOW < NCH:
            send_own(i + WINDOW)

    def distant(i):
        arrived(G.at[i, c, far, 0], grs.at[i, 2])
        arrived(G.at[i, c, far, 1], grs.at[i, 3])
        share(i, 3).start()

    def cols(y_, c_):
        return pl.ds(pl.multiple_of((c_ * NY + y_) * W, W), W)

    def halfcols(c_):
        return pl.ds(pl.multiple_of(c_ * NY * W, NY * W), NY * W)

    def piece(q_):
        return pl.ds(pl.multiple_of(q_ * E, E), E)

    def b_dst(n, q_):
        return XB.at[0, zl, piece(q_)] if n == 0 else B0.at[piece(q_)]

    def b_each(n, do):
        for s in range(2):
            b = (3 if n == 0 else 1) + s
            qd = y + NY * s
            for d in range(NY):
                yd = yy(d)
                src = rhs.at[b, piece(Q), cols(yd, c)]
                dst = b_dst(n, Q)

                def far_copy():
                    return remote(src, dst, bss.at[n, s, d], brs.at[n, Q], dev(yd, zl, qd, c))
                if d == 0:
                    if do == "start":
                        @pl.when(qd == Q)
                        def _():
                            pltpu.make_async_copy(src, dst, brs.at[n, Q]).start()

                    @pl.when(qd != Q)
                    def _():
                        far_copy().start() if do == "start" else far_copy().wait_send()
                else:
                    far_copy().start() if do == "start" else far_copy().wait_send()

    def b_wait(n):
        for q_ in range(NQ):
            arrived(b_dst(n, q_), brs.at[n, q_])

    def halfrows(h):
        return pl.ds(h * (T // 2), T // 2)

    def zmove(st, h):
        r = XB.at[st, zl, halfrows(h)]
        return remote(r, r, zss.at[st, h], zrs.at[st, h], dev(y, 1 - zl, Q, c))

    def split(st, k, h):
        v = XB[st, k, halfrows(h), :]
        hi = v.astype(jnp.bfloat16)
        lo = (v - hi.astype(jnp.float32)).astype(jnp.bfloat16)
        XS[st, k, halfrows(h), pl.ds(0, W)] = hi
        XS[st, k, halfrows(h), pl.ds(W, W)] = lo

    def zdone(st):
        for h in range(2):
            arrived(XB.at[st, 1 - zl, halfrows(h)], zrs.at[st, h])
            split(st, 1 - zl, h)

    def product(i, yb, st):
        total = None
        for k in range(2):
            a = G[i, k, yb].reshape(T, T)
            hi = a.astype(jnp.bfloat16)
            lo = (a - hi.astype(jnp.float32)).astype(jnp.bfloat16)
            x = XS[st, k]
            wide = jnp.dot(hi, x, preferred_element_type=jnp.float32)
            part = wide[:, :W] + wide[:, W:] + jnp.dot(
                lo, x[:, :W], preferred_element_type=jnp.float32)
            total = part if total is None else total + part
        return total

    def scatter(ph, t, h):
        return remote(PT.at[ph, t, h], RB.at[ph, Q, h], rss.at[ph, t, h], rrs.at[ph, Q, h],
                      dev(y, zl, t, c))

    def tiles(i, ph, st, lo, hi):
        h = i % 2

        def step(j, carry):
            yb = lax.rem(y + 3 + j, NY)
            total = product(i, yb, st)
            for s in range(2):
                t = NY * s + yb
                PT[ph, t, h] = total[s * (T // 2):(s + 1) * (T // 2)]

                @pl.when(t != Q)
                def _():
                    scatter(ph, t, h).start()
            return carry

        lax.fori_loop(lo, hi, step, 0)

    def gathered(ph, h):
        def step(d, total):
            src = qq(d)
            arrived(RB.at[ph, src, h], rrs.at[ph, src, h])
            return total + RB[ph, src, h]
        return lax.fori_loop(1, NQ, step, PT[ph, Q, h])

    def o_each(n, do):
        st = 1 if n == 1 else 3
        for d in range(NQ):
            qd = qq(d)
            src = XB.at[st, zl, piece(qd)]
            dst = out.at[1 + 2 * n + so, piece(qd), cols(y, c)]
            sem = ors.at[n, NY * so + y]

            def far_copy():
                return remote(src, dst, oss.at[n, d], sem, dev(yo, zl, qd, c))
            if d == 0:
                if do == "start":
                    @pl.when(home)
                    def _():
                        pltpu.make_async_copy(src, dst, sem).start()

                @pl.when(jnp.logical_not(home))
                def _():
                    far_copy().start() if do == "start" else far_copy().wait_send()
            else:
                far_copy().start() if do == "start" else far_copy().wait_send()

    def o_spread(n, s, d):
        r = out.at[1 + 2 * n + s, piece(Q), halfcols(c)]
        return remote(r, r, ess.at[n, s, d], ers.at[n, s, Q], dev(y, zl, qq(d), c))

    def o_turn(n, s):
        for yb in range(NY):
            arrived(out.at[1 + 2 * n + s, piece(Q), cols(yb, c)], ors.at[n, NY * s + yb])
        for d in range(1, NQ):
            o_spread(n, s, d).start()

    def o_share(n, s):
        r = out.at[1 + 2 * n + s, :, halfcols(c)]
        return remote(r, r, fss.at[n, s], frs.at[n, s], sib)

    def o_forward(n, s):
        for d in range(1, NQ):
            arrived(out.at[1 + 2 * n + s, piece(qq(d)), halfcols(c)], ers.at[n, s, qq(d)])
        o_share(n, s).start()

    send_own(0)
    b_each(0, "start")
    share(0, 0).start()
    locals_ = [pltpu.make_async_copy(own(i), blk(i, y), lsem.at[i]) for i in range(NCH)]
    rh_copy = pltpu.make_async_copy(rhs.at[0], RH, lsem.at[NCH])
    for cp in locals_:
        cp.start()
    rh_copy.start()
    own_up(0).wait_send()
    own_down(0).wait_send()
    send_own(1)
    share(1, 0).start()
    b_wait(0)
    for h in range(2):
        zmove(0, h).start()
        split(0, zl, h)
    near(0)
    for cp in locals_:
        cp.wait()
    rh_copy.wait()
    for i in range(2, NCH):
        share(i, 0).start()
    zdone(0)
    for j in range(3):
        wait_share(0, j)
    tiles(0, 0, 0, 0, 3)
    near(1)
    distant(0)
    wait_share(0, 3)
    tiles(0, 0, 0, 3, 4)
    for j in range(3):
        wait_share(1, j)
    tiles(1, 0, 0, 0, 3)
    distant(1)
    wait_share(1, 3)
    tiles(1, 0, 0, 3, 4)
    b_each(1, "start")

    def sent(ph):
        def step(d, carry):
            scatter(ph, qq(d), 0).wait_send()
            scatter(ph, qq(d), 1).wait_send()
            return carry
        lax.fori_loop(1, NQ, step, 0)

    def finish(ph, st, h):
        total = gathered(ph, h)
        if st == 2:
            XB[st, zl, halfrows(h), :] = B0[halfrows(h), :] - total
        else:
            XB[st, zl, halfrows(h), :] = total
        zmove(st, h).start()
        split(st, zl, h)

    def whole(i, ph, st):
        for j in range(4):
            wait_share(i, j)
        tiles(i, ph, st, 0, 4)

    near(2)
    finish(0, 1, 0)
    finish(0, 1, 1)
    o_each(1, "start")
    distant(2)
    zdone(1)
    whole(2, 1, 1)
    near(3)
    distant(3)
    whole(3, 1, 1)
    near(4)
    b_wait(1)
    distant(4)
    sent(1)
    o_turn(1, 0)
    finish(1, 2, 0)
    near(5)
    finish(1, 2, 1)
    o_turn(1, 1)
    zdone(2)
    whole(4, 2, 2)
    distant(5)
    whole(5, 2, 2)
    near(6)
    distant(6)
    near(7)
    o_forward(1, 0)
    o_forward(1, 1)
    for j in range(4):
        wait_share(6, j)

    def above_one(j, carry):
        yb = lax.rem(y + 3 + j, NY)
        PA[yb] = product(6, yb, 1)
        return carry
    lax.fori_loop(0, NY, above_one, 0)
    finish(2, 3, 0)
    finish(2, 3, 1)
    o_each(0, "start")
    distant(7)
    zdone(3)
    for j in range(4):
        wait_share(7, j)

    def above_two(j, carry):
        yb = lax.rem(y + 3 + j, NY)
        PA[yb] = PA[yb] + product(7, yb, 3)
        return carry
    lax.fori_loop(0, NY, above_two, 0)

    def a_each(do):
        for e in range(NY * NQ):
            yd, qd = yy(e // NQ), qq(e % NQ)
            src, dst = PA.at[yd, piece(qd)], RA.at[y, Q]
            if e == 0:
                if do == "start":
                    pltpu.make_async_copy(src, dst, ars.at[y]).start()
            else:
                far_copy = remote(src, dst, ass.at[e], ars.at[y], dev(yd, zl, qd, c))
                far_copy.start() if do == "start" else far_copy.wait_send()

    a_each("start")
    a_each("end")
    o_turn(0, 0)
    for yb in range(NY):
        arrived(RA.at[yb], ars.at[yb])
        total = RA[yb, 0]
        for q_ in range(1, NQ):
            total = total + RA[yb, q_]
        AB[piece(Q), cols(yb, c)] = total

    def a_part(q_, c_):
        return AB.at[piece(q_), halfcols(c_)]

    def a_spread(d):
        return remote(a_part(Q, c), a_part(Q, c), ess.at[2, 0, d], ers.at[2, 0, Q],
                      dev(y, zl, qq(d), c))

    def a_share(d):
        r = a_part(qq(d), c)
        return remote(r, r, yss.at[d], ars2.at[qq(d)], sib)

    for d in range(1, NQ):
        a_spread(d).start()
    a_share(0).start()
    o_turn(0, 1)
    o_forward(0, 0)
    for d in range(1, NQ):
        arrived(a_part(qq(d), c), ers.at[2, 0, qq(d)])
        a_share(d).start()
    out[0, :, halfcols(c)] = RH[:, halfcols(c)] - AB[:, halfcols(c)]
    o_forward(0, 1)
    for d in range(NQ):
        arrived(a_part(qq(d), 1 - c), ars2.at[qq(d)])
    out[0, :, halfcols(1 - c)] = RH[:, halfcols(1 - c)] - AB[:, halfcols(1 - c)]

    for n in range(2):
        for s in range(2):
            arrived(out.at[1 + 2 * n + s, :, halfcols(1 - c)], frs.at[n, s])
    for i in range(NCH):
        if i:
            own_up(i).wait_send()
            own_down(i).wait_send()
        relay_up(i).wait_send()
        relay_down(i).wait_send()
        for j in range(4):
            share(i, j).wait_send()
    sent(0)
    sent(2)
    for st in range(4):
        zmove(st, 0).wait_send()
        zmove(st, 1).wait_send()
    for n in range(2):
        b_each(n, "end")
        o_each(n, "end")
        for d in range(1, NQ):
            o_spread(n, 0, d).wait_send()
            o_spread(n, 1, d).wait_send()
        for s in range(2):
            o_share(n, s).wait_send()
    for d in range(1, NQ):
        a_spread(d).wait_send()
    for d in range(NQ):
        a_share(d).wait_send()


def shards(factor, inverse, rhs):
    f32, bf16 = jnp.float32, jnp.bfloat16
    dma = pltpu.SemaphoreType.DMA
    solved = pl.pallas_call(
        kernel,
        out_shape=pltpu.VMEM((5, T, NQ * W), f32),
        in_specs=[pl.BlockSpec(memory_space=pltpu.HBM)] * 3,
        out_specs=pl.BlockSpec(memory_space=pltpu.VMEM),
        scratch_shapes=[
            pltpu.VMEM((NCH, 2, NY, 2, T // 2, T), f32),
            pltpu.VMEM((3, NQ, 2, T // 2, W), f32),
            pltpu.VMEM((3, NQ, 2, T // 2, W), f32),
            pltpu.VMEM((4, 2, T, W), f32),
            pltpu.VMEM((4, 2, T, 2 * W), bf16),
            pltpu.VMEM((T, W), f32),
            pltpu.VMEM((NY, T, W), f32),
            pltpu.VMEM((NY, NQ, E, W), f32),
            pltpu.VMEM((T, NQ * W), f32),
            pltpu.VMEM((T, NQ * W), f32),
            dma((NCH + 1,)),
            dma((2, 2, NY)), dma((2, NQ)),
            dma((NCH, 4)), dma((NCH, 4)),
            dma((NCH, 4)), dma((NCH, 4)),
            dma((3, NQ, 2)), dma((3, NQ, 2)),
            dma((NY * NQ,)), dma((NY,)),
            dma((4, 2)), dma((4, 2)),
            dma((2, NQ)), dma((2, NQ)),
            dma((3, 2, NQ)), dma((3, 2, NQ)),
            dma((2, 2)), dma((2, 2)),
            dma((NQ,)), dma((NQ,)),
        ],
        compiler_params=pltpu.CompilerParams(
            collective_id=0, has_side_effects=True, vmem_limit_bytes=56 * 2**20),
        name="panel_steps",
    )(factor.reshape(5, 2, T // 2, 2 * T), inverse.reshape(2, 2, 2, T // 2, T),
      rhs.reshape(5, T, NQ * W))
    return solved.reshape(rhs.shape)


def solution(mesh):
    return jax.shard_map(
        shards,
        mesh=mesh,
        in_specs=(P("row", "col"), P(None, "row", "col"), P("row", None)),
        out_specs=P("row", None),
        check_vma=False,
    )
```

```python
import functools

import jax
import jax.numpy as jnp
from jax import lax
from jax.experimental import pallas as pl
from jax.experimental.pallas import tpu as pltpu
from jax.sharding import PartitionSpec as P

MESH = pl.DeviceIdType.MESH
T = 256
W = 128
NY = 4
NQ = 8
NCH = 8
E = 32
WINDOW = 2


def kernel(fac, inv, rhs, out,
           G, PT, RB, XB, XS, B0, PA, RA, AB, RH,
           lsem, bss, brs, gss, grs, dss, drs, rss, rrs, ass, ars,
           zss, zrs, oss, ors, ess, ers, fss, frs, yss, ars2):
    row = lax.axis_index("row")
    col = lax.axis_index("col")
    y, zl = lax.div(row, 2), lax.rem(row, 2)
    Q, c = lax.div(col, 2), lax.rem(col, 2)
    yo, so = lax.rem(Q, NY), lax.div(Q, NY)

    def dev(y_, zl_, q_, c_):
        return (2 * y_ + zl_, 2 * q_ + c_)

    def yy(d):
        return lax.rem(y + d, NY)

    def qq(d):
        return lax.rem(Q + d, NQ)

    up, down, far = yy(1), yy(3), yy(2)
    home = y == yo
    sib = dev(y, zl, Q, 1 - c)

    def remote(src, dst, ssem, rsem, device):
        return pltpu.make_async_remote_copy(
            src_ref=src, dst_ref=dst, send_sem=ssem, recv_sem=rsem,
            device_id=device, device_id_type=MESH)

    def arrived(r, sem):
        pltpu.make_async_copy(r, r, sem).wait()

    def signal(device):
        pl.semaphore_signal(bar, inc=1, device_id=device, device_id_type=MESH)

    bar = pltpu.get_barrier_semaphore()
    for e in range(1, NY * NQ):
        signal(dev(yy(e // NQ), zl, qq(e % NQ), c))
    signal(sib)
    signal(dev(y, 1 - zl, Q, c))
    pl.semaphore_wait(bar, NY * NQ + 1)

    def own(i):
        if i < 2:
            return inv.at[1, :, i]
        if i < 4:
            return fac.at[pl.ds(1, 2), i - 2, :, pl.ds(T, T)]
        if i < 6:
            return inv.at[0, :, i - 4]
        if i == 6:
            return fac.at[0, :, :, pl.ds(T, T)]
        return fac.at[0, :, :, pl.ds(0, T)]

    def blk(i, yb):
        return G.at[i, c, yb]

    def own_up(i):
        return remote(own(i), blk(i, y), gss.at[i, 0], grs.at[i, 0], dev(up, zl, Q, c))

    def own_down(i):
        return remote(own(i), blk(i, y), gss.at[i, 1], grs.at[i, 1], dev(down, zl, Q, c))

    def relay_up(i):
        r = G.at[i, c, down, 0]
        return remote(r, r, gss.at[i, 2], grs.at[i, 2], dev(up, zl, Q, c))

    def relay_down(i):
        r = G.at[i, c, up, 1]
        return remote(r, r, gss.at[i, 3], grs.at[i, 3], dev(down, zl, Q, c))

    def share(i, j):
        yb = (y, down, up, far)[j]
        src = own(i) if j == 0 else blk(i, yb)
        return remote(src, blk(i, yb), dss.at[i, j], drs.at[i, j], sib)

    def wait_share(i, j):
        yb = (y, down, up, far)[j]
        arrived(G.at[i, 1 - c, yb], drs.at[i, j])

    def send_own(i):
        own_up(i).start()
        own_down(i).start()

    def near(i):
        arrived(blk(i, down), grs.at[i, 0])
        relay_up(i).start()
        arrived(blk(i, up), grs.at[i, 1])
        relay_down(i).start()
        share(i, 1).start()
        share(i, 2).start()
        if i + WINDOW < NCH:
            send_own(i + WINDOW)

    def distant(i):
        arrived(G.at[i, c, far, 0], grs.at[i, 2])
        arrived(G.at[i, c, far, 1], grs.at[i, 3])
        share(i, 3).start()

    def cols(y_, c_):
        return pl.ds(pl.multiple_of((c_ * NY + y_) * W, W), W)

    def halfcols(c_):
        return pl.ds(pl.multiple_of(c_ * NY * W, NY * W), NY * W)

    def piece(q_):
        return pl.ds(pl.multiple_of(q_ * E, E), E)

    def b_dst(n, q_):
        return XB.at[0, zl, piece(q_)] if n == 0 else B0.at[piece(q_)]

    def b_each(n, do):
        for s in range(2):
            b = (3 if n == 0 else 1) + s
            qd = y + NY * s
            for d in range(NY):
                yd = yy(d)
                src = rhs.at[b, piece(Q), cols(yd, c)]
                dst = b_dst(n, Q)

                def far_copy():
                    return remote(src, dst, bss.at[n, s, d], brs.at[n, Q], dev(yd, zl, qd, c))
                if d == 0:
                    if do == "start":
                        @pl.when(qd == Q)
                        def _():
                            pltpu.make_async_copy(src, dst, brs.at[n, Q]).start()

                    @pl.when(qd != Q)
                    def _():
                        far_copy().start() if do == "start" else far_copy().wait_send()
                else:
                    far_copy().start() if do == "start" else far_copy().wait_send()

    def b_wait(n):
        for q_ in range(NQ):
            arrived(b_dst(n, q_), brs.at[n, q_])

    def halfrows(h):
        return pl.ds(h * (T // 2), T // 2)

    def zmove(st, h):
        r = XB.at[st, zl, halfrows(h)]
        return remote(r, r, zss.at[st, h], zrs.at[st, h], dev(y, 1 - zl, Q, c))

    def split(st, k, h):
        v = XB[st, k, halfrows(h), :]
        hi = v.astype(jnp.bfloat16)
        lo = (v - hi.astype(jnp.float32)).astype(jnp.bfloat16)
        XS[st, k, halfrows(h), pl.ds(0, W)] = hi
        XS[st, k, halfrows(h), pl.ds(W, W)] = lo

    def zdone(st):
        for h in range(2):
            arrived(XB.at[st, 1 - zl, halfrows(h)], zrs.at[st, h])
            split(st, 1 - zl, h)

    def product(i, yb, st):
        total = None
        for k in range(2):
            a = G[i, k, yb].reshape(T, T)
            hi = a.astype(jnp.bfloat16)
            lo = (a - hi.astype(jnp.float32)).astype(jnp.bfloat16)
            x = XS[st, k]
            wide = jnp.dot(hi, x, preferred_element_type=jnp.float32)
            part = wide[:, :W] + wide[:, W:] + jnp.dot(
                lo, x[:, :W], preferred_element_type=jnp.float32)
            total = part if total is None else total + part
        return total

    def scatter(ph, t, h):
        return remote(PT.at[ph, t, h], RB.at[ph, Q, h], rss.at[ph, t, h], rrs.at[ph, Q, h],
                      dev(y, zl, t, c))

    def tiles(i, ph, st, lo, hi):
        h = i % 2

        def step(j, carry):
            yb = lax.rem(y + 3 + j, NY)
            total = product(i, yb, st)
            for s in range(2):
                t = NY * s + yb
                PT[ph, t, h] = total[s * (T // 2):(s + 1) * (T // 2)]

                @pl.when(t != Q)
                def _():
                    scatter(ph, t, h).start()
            return carry

        lax.fori_loop(lo, hi, step, 0)

    def gathered(ph, h):
        def step(d, total):
            src = qq(d)
            arrived(RB.at[ph, src, h], rrs.at[ph, src, h])
            return total + RB[ph, src, h]
        return lax.fori_loop(1, NQ, step, PT[ph, Q, h])

    def o_each(n, do):
        st = 1 if n == 1 else 3
        for d in range(NQ):
            qd = qq(d)
            src = XB.at[st, zl, piece(qd)]
            dst = out.at[1 + 2 * n + so, piece(qd), cols(y, c)]
            sem = ors.at[n, NY * so + y]

            def far_copy():
                return remote(src, dst, oss.at[n, d], sem, dev(yo, zl, qd, c))
            if d == 0:
                if do == "start":
                    @pl.when(home)
                    def _():
                        pltpu.make_async_copy(src, dst, sem).start()

                @pl.when(jnp.logical_not(home))
                def _():
                    far_copy().start() if do == "start" else far_copy().wait_send()
            else:
                far_copy().start() if do == "start" else far_copy().wait_send()

    def o_spread(n, s, d):
        r = out.at[1 + 2 * n + s, piece(Q), halfcols(c)]
        return remote(r, r, ess.at[n, s, d], ers.at[n, s, Q], dev(y, zl, qq(d), c))

    def o_turn(n, s):
        for yb in range(NY):
            arrived(out.at[1 + 2 * n + s, piece(Q), cols(yb, c)], ors.at[n, NY * s + yb])
        for d in range(1, NQ):
            o_spread(n, s, d).start()

    def o_share(n, s):
        r = out.at[1 + 2 * n + s, :, halfcols(c)]
        return remote(r, r, fss.at[n, s], frs.at[n, s], sib)

    def o_forward(n, s):
        for d in range(1, NQ):
            arrived(out.at[1 + 2 * n + s, piece(qq(d)), halfcols(c)], ers.at[n, s, qq(d)])
        o_share(n, s).start()

    send_own(0)
    b_each(0, "start")
    share(0, 0).start()
    locals_ = [pltpu.make_async_copy(own(i), blk(i, y), lsem.at[i]) for i in range(NCH)]
    rh_copy = pltpu.make_async_copy(rhs.at[0], RH, lsem.at[NCH])
    for cp in locals_:
        cp.start()
    rh_copy.start()
    own_up(0).wait_send()
    own_down(0).wait_send()
    send_own(1)
    share(1, 0).start()
    b_wait(0)
    for h in range(2):
        zmove(0, h).start()
        split(0, zl, h)
    near(0)
    for cp in locals_:
        cp.wait()
    rh_copy.wait()
    for i in range(2, NCH):
        share(i, 0).start()
    zdone(0)
    for j in range(3):
        wait_share(0, j)
    tiles(0, 0, 0, 0, 3)
    near(1)
    distant(0)
    wait_share(0, 3)
    tiles(0, 0, 0, 3, 4)
    for j in range(3):
        wait_share(1, j)
    tiles(1, 0, 0, 0, 3)
    distant(1)
    wait_share(1, 3)
    tiles(1, 0, 0, 3, 4)
    b_each(1, "start")

    def sent(ph):
        def step(d, carry):
            scatter(ph, qq(d), 0).wait_send()
            scatter(ph, qq(d), 1).wait_send()
            return carry
        lax.fori_loop(1, NQ, step, 0)

    def finish(ph, st, h):
        total = gathered(ph, h)
        if st == 2:
            XB[st, zl, halfrows(h), :] = B0[halfrows(h), :] - total
        else:
            XB[st, zl, halfrows(h), :] = total
        zmove(st, h).start()
        split(st, zl, h)

    def whole(i, ph, st):
        for j in range(4):
            wait_share(i, j)
        tiles(i, ph, st, 0, 4)

    near(2)
    finish(0, 1, 0)
    finish(0, 1, 1)
    o_each(1, "start")
    distant(2)
    zdone(1)
    whole(2, 1, 1)
    near(3)
    distant(3)
    whole(3, 1, 1)
    near(4)
    b_wait(1)
    distant(4)
    sent(1)
    o_turn(1, 0)
    finish(1, 2, 0)
    near(5)
    finish(1, 2, 1)
    o_turn(1, 1)
    zdone(2)
    whole(4, 2, 2)
    distant(5)
    whole(5, 2, 2)
    near(6)
    distant(6)
    near(7)
    o_forward(1, 0)
    o_forward(1, 1)
    for j in range(4):
        wait_share(6, j)

    def above_one(j, carry):
        yb = lax.rem(y + 3 + j, NY)
        PA[yb] = product(6, yb, 1)
        return carry
    lax.fori_loop(0, NY, above_one, 0)
    finish(2, 3, 0)
    finish(2, 3, 1)
    o_each(0, "start")
    distant(7)
    zdone(3)
    for j in range(4):
        wait_share(7, j)

    def above_two(j, carry):
        yb = lax.rem(y + 3 + j, NY)
        PA[yb] = PA[yb] + product(7, yb, 3)
        return carry
    lax.fori_loop(0, NY, above_two, 0)

    def a_each(do):
        for e in range(NY * NQ):
            yd, qd = yy(e // NQ), qq(e % NQ)
            src, dst = PA.at[yd, piece(qd)], RA.at[y, Q]
            if e == 0:
                if do == "start":
                    pltpu.make_async_copy(src, dst, ars.at[y]).start()
            else:
                far_copy = remote(src, dst, ass.at[e], ars.at[y], dev(yd, zl, qd, c))
                far_copy.start() if do == "start" else far_copy.wait_send()

    a_each("start")
    o_turn(0, 0)
    for yb in range(NY):
        arrived(RA.at[yb], ars.at[yb])
        total = RA[yb, 0]
        for q_ in range(1, NQ):
            total = total + RA[yb, q_]
        AB[piece(Q), cols(yb, c)] = total

    def a_part(q_, c_):
        return AB.at[piece(q_), halfcols(c_)]

    def a_spread(d):
        return remote(a_part(Q, c), a_part(Q, c), ess.at[2, 0, d], ers.at[2, 0, Q],
                      dev(y, zl, qq(d), c))

    def a_share(d):
        r = a_part(qq(d), c)
        return remote(r, r, yss.at[d], ars2.at[qq(d)], sib)

    for d in range(1, NQ):
        a_spread(d).start()
    a_share(0).start()
    o_turn(0, 1)
    o_forward(0, 0)
    for d in range(1, NQ):
        arrived(a_part(qq(d), c), ers.at[2, 0, qq(d)])
        a_share(d).start()
    out[0, :, halfcols(c)] = RH[:, halfcols(c)] - AB[:, halfcols(c)]
    o_forward(0, 1)
    for d in range(NQ):
        arrived(a_part(qq(d), 1 - c), ars2.at[qq(d)])
    out[0, :, halfcols(1 - c)] = RH[:, halfcols(1 - c)] - AB[:, halfcols(1 - c)]

    a_each("end")
    for n in range(2):
        for s in range(2):
            arrived(out.at[1 + 2 * n + s, :, halfcols(1 - c)], frs.at[n, s])
    for i in range(NCH):
        if i:
            own_up(i).wait_send()
            own_down(i).wait_send()
        relay_up(i).wait_send()
        relay_down(i).wait_send()
        for j in range(4):
            share(i, j).wait_send()
    sent(0)
    sent(2)
    for st in range(4):
        zmove(st, 0).wait_send()
        zmove(st, 1).wait_send()
    for n in range(2):
        b_each(n, "end")
        o_each(n, "end")
        for d in range(1, NQ):
            o_spread(n, 0, d).wait_send()
            o_spread(n, 1, d).wait_send()
        for s in range(2):
            o_share(n, s).wait_send()
    for d in range(1, NQ):
        a_spread(d).wait_send()
    for d in range(NQ):
        a_share(d).wait_send()


def shards(factor, inverse, rhs):
    f32, bf16 = jnp.float32, jnp.bfloat16
    dma = pltpu.SemaphoreType.DMA
    solved = pl.pallas_call(
        kernel,
        out_shape=pltpu.VMEM((5, T, NQ * W), f32),
        in_specs=[pl.BlockSpec(memory_space=pltpu.HBM)] * 3,
        out_specs=pl.BlockSpec(memory_space=pltpu.VMEM),
        scratch_shapes=[
            pltpu.VMEM((NCH, 2, NY, 2, T // 2, T), f32),
            pltpu.VMEM((3, NQ, 2, T // 2, W), f32),
            pltpu.VMEM((3, NQ, 2, T // 2, W), f32),
            pltpu.VMEM((4, 2, T, W), f32),
            pltpu.VMEM((4, 2, T, 2 * W), bf16),
            pltpu.VMEM((T, W), f32),
            pltpu.VMEM((NY, T, W), f32),
            pltpu.VMEM((NY, NQ, E, W), f32),
            pltpu.VMEM((T, NQ * W), f32),
            pltpu.VMEM((T, NQ * W), f32),
            dma((NCH + 1,)),
            dma((2, 2, NY)), dma((2, NQ)),
            dma((NCH, 4)), dma((NCH, 4)),
            dma((NCH, 4)), dma((NCH, 4)),
            dma((3, NQ, 2)), dma((3, NQ, 2)),
            dma((NY * NQ,)), dma((NY,)),
            dma((4, 2)), dma((4, 2)),
            dma((2, NQ)), dma((2, NQ)),
            dma((3, 2, NQ)), dma((3, 2, NQ)),
            dma((2, 2)), dma((2, 2)),
            dma((NQ,)), dma((NQ,)),
        ],
        compiler_params=pltpu.CompilerParams(
            collective_id=0, has_side_effects=True, vmem_limit_bytes=56 * 2**20),
        name="panel_steps",
    )(factor.reshape(5, 2, T // 2, 2 * T), inverse.reshape(2, 2, 2, T // 2, T),
      rhs.reshape(5, T, NQ * W))
    return solved.reshape(rhs.shape)


def solution(mesh):
    return jax.shard_map(
        shards,
        mesh=mesh,
        in_specs=(P("row", "col"), P(None, "row", "col"), P("row", None)),
        out_specs=P("row", None),
        check_vma=False,
    )
```

```python
import functools

import jax
import jax.numpy as jnp
from jax import lax
from jax.experimental import pallas as pl
from jax.experimental.pallas import tpu as pltpu
from jax.sharding import PartitionSpec as P

MESH = pl.DeviceIdType.MESH
T = 256
W = 128
NY = 4
NQ = 8
NCH = 8
E = 32
WINDOW = 2


def kernel(fac, inv, rhs, out,
           G, PT, RB, XB, XS, B0, PA, RA, AB, RH,
           lsem, bss, brs, gss, grs, dss, drs, rss, rrs, ass, ars,
           zss, zrs, oss, ors, ess, ers, fss, frs, yss, ars2):
    row = lax.axis_index("row")
    col = lax.axis_index("col")
    y, zl = lax.div(row, 2), lax.rem(row, 2)
    Q, c = lax.div(col, 2), lax.rem(col, 2)
    yo, so = lax.rem(Q, NY), lax.div(Q, NY)

    def dev(y_, zl_, q_, c_):
        return (2 * y_ + zl_, 2 * q_ + c_)

    def yy(d):
        return lax.rem(y + d, NY)

    def qq(d):
        return lax.rem(Q + d, NQ)

    up, down, far = yy(1), yy(3), yy(2)
    home = y == yo
    sib = dev(y, zl, Q, 1 - c)

    def remote(src, dst, ssem, rsem, device):
        return pltpu.make_async_remote_copy(
            src_ref=src, dst_ref=dst, send_sem=ssem, recv_sem=rsem,
            device_id=device, device_id_type=MESH)

    def arrived(r, sem):
        pltpu.make_async_copy(r, r, sem).wait()

    def signal(device):
        pl.semaphore_signal(bar, inc=1, device_id=device, device_id_type=MESH)

    bar = pltpu.get_barrier_semaphore()
    for e in range(1, NY * NQ):
        signal(dev(yy(e // NQ), zl, qq(e % NQ), c))
    signal(sib)
    signal(dev(y, 1 - zl, Q, c))
    pl.semaphore_wait(bar, NY * NQ + 1)

    def own(i):
        if i < 2:
            return inv.at[1, :, i]
        if i < 4:
            return fac.at[pl.ds(1, 2), i - 2, :, pl.ds(T, T)]
        if i < 6:
            return inv.at[0, :, i - 4]
        if i == 6:
            return fac.at[0, :, :, pl.ds(T, T)]
        return fac.at[0, :, :, pl.ds(0, T)]

    def blk(i, yb):
        return G.at[i, c, yb]

    def own_up(i):
        return remote(own(i), blk(i, y), gss.at[i, 0], grs.at[i, 0], dev(up, zl, Q, c))

    def own_down(i):
        return remote(own(i), blk(i, y), gss.at[i, 1], grs.at[i, 1], dev(down, zl, Q, c))

    def relay_up(i):
        r = G.at[i, c, down, 0]
        return remote(r, r, gss.at[i, 2], grs.at[i, 2], dev(up, zl, Q, c))

    def relay_down(i):
        r = G.at[i, c, up, 1]
        return remote(r, r, gss.at[i, 3], grs.at[i, 3], dev(down, zl, Q, c))

    def share(i, j):
        yb = (y, down, up, far)[j]
        src = own(i) if j == 0 else blk(i, yb)
        return remote(src, blk(i, yb), dss.at[i, j], drs.at[i, j], sib)

    def wait_share(i, j):
        yb = (y, down, up, far)[j]
        arrived(G.at[i, 1 - c, yb], drs.at[i, j])

    def send_own(i):
        own_up(i).start()
        own_down(i).start()

    def near(i):
        arrived(blk(i, down), grs.at[i, 0])
        relay_up(i).start()
        arrived(blk(i, up), grs.at[i, 1])
        relay_down(i).start()
        share(i, 1).start()
        share(i, 2).start()
        if i + WINDOW < NCH:
            send_own(i + WINDOW)

    def distant(i):
        arrived(G.at[i, c, far, 0], grs.at[i, 2])
        arrived(G.at[i, c, far, 1], grs.at[i, 3])
        share(i, 3).start()

    def cols(y_, c_):
        return pl.ds(pl.multiple_of((c_ * NY + y_) * W, W), W)

    def halfcols(c_):
        return pl.ds(pl.multiple_of(c_ * NY * W, NY * W), NY * W)

    def piece(q_):
        return pl.ds(pl.multiple_of(q_ * E, E), E)

    def b_dst(n, q_):
        return XB.at[0, zl, piece(q_)] if n == 0 else B0.at[piece(q_)]

    def b_each(n, do):
        for s in range(2):
            b = (3 if n == 0 else 1) + s
            qd = y + NY * s
            for d in range(NY):
                yd = yy(d)
                src = rhs.at[b, piece(Q), cols(yd, c)]
                dst = b_dst(n, Q)

                def far_copy():
                    return remote(src, dst, bss.at[n, s, d], brs.at[n, Q], dev(yd, zl, qd, c))
                if d == 0:
                    if do == "start":
                        @pl.when(qd == Q)
                        def _():
                            pltpu.make_async_copy(src, dst, brs.at[n, Q]).start()

                    @pl.when(qd != Q)
                    def _():
                        far_copy().start() if do == "start" else far_copy().wait_send()
                else:
                    far_copy().start() if do == "start" else far_copy().wait_send()

    def b_wait(n):
        for q_ in range(NQ):
            arrived(b_dst(n, q_), brs.at[n, q_])

    def halfrows(h):
        return pl.ds(h * (T // 2), T // 2)

    def zmove(st, h):
        r = XB.at[st, zl, halfrows(h)]
        return remote(r, r, zss.at[st, h], zrs.at[st, h], dev(y, 1 - zl, Q, c))

    def split(st, k, h):
        v = XB[st, k, halfrows(h), :]
        hi = v.astype(jnp.bfloat16)
        lo = (v - hi.astype(jnp.float32)).astype(jnp.bfloat16)
        XS[st, k, halfrows(h), pl.ds(0, W)] = hi
        XS[st, k, halfrows(h), pl.ds(W, W)] = lo

    def zdone(st):
        for h in range(2):
            arrived(XB.at[st, 1 - zl, halfrows(h)], zrs.at[st, h])
            split(st, 1 - zl, h)

    def product(i, yb, st):
        total = None
        for k in range(2):
            a = G[i, k, yb].reshape(T, T)
            hi = a.astype(jnp.bfloat16)
            lo = (a - hi.astype(jnp.float32)).astype(jnp.bfloat16)
            x = XS[st, k]
            wide = jnp.dot(hi, x, preferred_element_type=jnp.float32)
            part = wide[:, :W] + wide[:, W:] + jnp.dot(
                lo, x[:, :W], preferred_element_type=jnp.float32)
            total = part if total is None else total + part
        return total

    def scatter(ph, t, h):
        return remote(PT.at[ph, t, h], RB.at[ph, Q, h], rss.at[ph, t, h], rrs.at[ph, Q, h],
                      dev(y, zl, t, c))

    def tiles(i, ph, st, lo, hi):
        h = i % 2

        def step(j, carry):
            yb = lax.rem(y + 3 + j, NY)
            total = product(i, yb, st)
            for s in range(2):
                t = NY * s + yb
                PT[ph, t, h] = total[s * (T // 2):(s + 1) * (T // 2)]

                @pl.when(t != Q)
                def _():
                    scatter(ph, t, h).start()
            return carry

        lax.fori_loop(lo, hi, step, 0)

    def gathered(ph, h):
        total = PT[ph, Q, h]
        for d in range(1, NQ):
            src = qq(d)
            arrived(RB.at[ph, src, h], rrs.at[ph, src, h])
            total = total + RB[ph, src, h]
        return total

    def o_each(n, do):
        st = 1 if n == 1 else 3
        for d in range(NQ):
            qd = qq(d)
            src = XB.at[st, zl, piece(qd)]
            dst = out.at[1 + 2 * n + so, piece(qd), cols(y, c)]
            sem = ors.at[n, NY * so + y]

            def far_copy():
                return remote(src, dst, oss.at[n, d], sem, dev(yo, zl, qd, c))
            if d == 0:
                if do == "start":
                    @pl.when(home)
                    def _():
                        pltpu.make_async_copy(src, dst, sem).start()

                @pl.when(jnp.logical_not(home))
                def _():
                    far_copy().start() if do == "start" else far_copy().wait_send()
            else:
                far_copy().start() if do == "start" else far_copy().wait_send()

    def o_spread(n, s, d):
        r = out.at[1 + 2 * n + s, piece(Q), halfcols(c)]
        return remote(r, r, ess.at[n, s, d], ers.at[n, s, Q], dev(y, zl, qq(d), c))

    def o_turn(n, s):
        for yb in range(NY):
            arrived(out.at[1 + 2 * n + s, piece(Q), cols(yb, c)], ors.at[n, NY * s + yb])
        for d in range(1, NQ):
            o_spread(n, s, d).start()

    def o_share(n, s):
        r = out.at[1 + 2 * n + s, :, halfcols(c)]
        return remote(r, r, fss.at[n, s], frs.at[n, s], sib)

    def o_forward(n, s):
        for d in range(1, NQ):
            arrived(out.at[1 + 2 * n + s, piece(qq(d)), halfcols(c)], ers.at[n, s, qq(d)])
        o_share(n, s).start()

    send_own(0)
    b_each(0, "start")
    share(0, 0).start()
    locals_ = [pltpu.make_async_copy(own(i), blk(i, y), lsem.at[i]) for i in range(NCH)]
    rh_copy = pltpu.make_async_copy(rhs.at[0], RH, lsem.at[NCH])
    for cp in locals_:
        cp.start()
    rh_copy.start()
    own_up(0).wait_send()
    own_down(0).wait_send()
    send_own(1)
    share(1, 0).start()
    b_wait(0)
    for h in range(2):
        zmove(0, h).start()
        split(0, zl, h)
    near(0)
    for cp in locals_:
        cp.wait()
    rh_copy.wait()
    for i in range(2, NCH):
        share(i, 0).start()
    zdone(0)
    for j in range(3):
        wait_share(0, j)
    tiles(0, 0, 0, 0, 3)
    near(1)
    distant(0)
    wait_share(0, 3)
    tiles(0, 0, 0, 3, 4)
    for j in range(3):
        wait_share(1, j)
    tiles(1, 0, 0, 0, 3)
    distant(1)
    wait_share(1, 3)
    tiles(1, 0, 0, 3, 4)
    b_each(1, "start")

    def sent(ph):
        def step(d, carry):
            scatter(ph, qq(d), 0).wait_send()
            scatter(ph, qq(d), 1).wait_send()
            return carry
        lax.fori_loop(1, NQ, step, 0)

    def finish(ph, st, h):
        total = gathered(ph, h)
        if st == 2:
            XB[st, zl, halfrows(h), :] = B0[halfrows(h), :] - total
        else:
            XB[st, zl, halfrows(h), :] = total
        zmove(st, h).start()
        split(st, zl, h)

    def whole(i, ph, st):
        for j in range(4):
            wait_share(i, j)
        tiles(i, ph, st, 0, 4)

    near(2)
    finish(0, 1, 0)
    finish(0, 1, 1)
    o_each(1, "start")
    distant(2)
    zdone(1)
    whole(2, 1, 1)
    near(3)
    distant(3)
    whole(3, 1, 1)
    near(4)
    b_wait(1)
    distant(4)
    sent(1)
    o_turn(1, 0)
    finish(1, 2, 0)
    near(5)
    finish(1, 2, 1)
    o_turn(1, 1)
    zdone(2)
    whole(4, 2, 2)
    distant(5)
    whole(5, 2, 2)
    near(6)
    distant(6)
    near(7)
    o_forward(1, 0)
    o_forward(1, 1)
    for j in range(4):
        wait_share(6, j)

    def above_one(j, carry):
        yb = lax.rem(y + 3 + j, NY)
        PA[yb] = product(6, yb, 1)
        return carry
    lax.fori_loop(0, NY, above_one, 0)
    finish(2, 3, 0)
    finish(2, 3, 1)
    o_each(0, "start")
    distant(7)
    zdone(3)
    for j in range(4):
        wait_share(7, j)

    def above_two(j, carry):
        yb = lax.rem(y + 3 + j, NY)
        PA[yb] = PA[yb] + product(7, yb, 3)
        return carry
    lax.fori_loop(0, NY, above_two, 0)

    def a_each(do):
        for e in range(NY * NQ):
            yd, qd = yy(e // NQ), qq(e % NQ)
            src, dst = PA.at[yd, piece(qd)], RA.at[y, Q]
            if e == 0:
                if do == "start":
                    pltpu.make_async_copy(src, dst, ars.at[y]).start()
            else:
                far_copy = remote(src, dst, ass.at[e], ars.at[y], dev(yd, zl, qd, c))
                far_copy.start() if do == "start" else far_copy.wait_send()

    a_each("start")
    o_turn(0, 0)
    for yb in range(NY):
        arrived(RA.at[yb], ars.at[yb])
        total = RA[yb, 0]
        for q_ in range(1, NQ):
            total = total + RA[yb, q_]
        AB[piece(Q), cols(yb, c)] = total

    def a_part(q_, c_):
        return AB.at[piece(q_), halfcols(c_)]

    def a_spread(d):
        return remote(a_part(Q, c), a_part(Q, c), ess.at[2, 0, d], ers.at[2, 0, Q],
                      dev(y, zl, qq(d), c))

    def a_share(d):
        r = a_part(qq(d), c)
        return remote(r, r, yss.at[d], ars2.at[qq(d)], sib)

    for d in range(1, NQ):
        a_spread(d).start()
    a_share(0).start()
    o_turn(0, 1)
    o_forward(0, 0)
    for d in range(1, NQ):
        arrived(a_part(qq(d), c), ers.at[2, 0, qq(d)])
        a_share(d).start()
    out[0, :, halfcols(c)] = RH[:, halfcols(c)] - AB[:, halfcols(c)]
    o_forward(0, 1)
    for d in range(NQ):
        arrived(a_part(qq(d), 1 - c), ars2.at[qq(d)])
    out[0, :, halfcols(1 - c)] = RH[:, halfcols(1 - c)] - AB[:, halfcols(1 - c)]

    a_each("end")
    for n in range(2):
        for s in range(2):
            arrived(out.at[1 + 2 * n + s, :, halfcols(1 - c)], frs.at[n, s])
    for i in range(NCH):
        if i:
            own_up(i).wait_send()
            own_down(i).wait_send()
        relay_up(i).wait_send()
        relay_down(i).wait_send()
        for j in range(4):
            share(i, j).wait_send()
    sent(0)
    sent(2)
    for st in range(4):
        zmove(st, 0).wait_send()
        zmove(st, 1).wait_send()
    for n in range(2):
        b_each(n, "end")
        o_each(n, "end")
        for d in range(1, NQ):
            o_spread(n, 0, d).wait_send()
            o_spread(n, 1, d).wait_send()
        for s in range(2):
            o_share(n, s).wait_send()
    for d in range(1, NQ):
        a_spread(d).wait_send()
    for d in range(NQ):
        a_share(d).wait_send()


def shards(factor, inverse, rhs):
    f32, bf16 = jnp.float32, jnp.bfloat16
    dma = pltpu.SemaphoreType.DMA
    solved = pl.pallas_call(
        kernel,
        out_shape=pltpu.VMEM((5, T, NQ * W), f32),
        in_specs=[pl.BlockSpec(memory_space=pltpu.HBM)] * 3,
        out_specs=pl.BlockSpec(memory_space=pltpu.VMEM),
        scratch_shapes=[
            pltpu.VMEM((NCH, 2, NY, 2, T // 2, T), f32),
            pltpu.VMEM((3, NQ, 2, T // 2, W), f32),
            pltpu.VMEM((3, NQ, 2, T // 2, W), f32),
            pltpu.VMEM((4, 2, T, W), f32),
            pltpu.VMEM((4, 2, T, 2 * W), bf16),
            pltpu.VMEM((T, W), f32),
            pltpu.VMEM((NY, T, W), f32),
            pltpu.VMEM((NY, NQ, E, W), f32),
            pltpu.VMEM((T, NQ * W), f32),
            pltpu.VMEM((T, NQ * W), f32),
            dma((NCH + 1,)),
            dma((2, 2, NY)), dma((2, NQ)),
            dma((NCH, 4)), dma((NCH, 4)),
            dma((NCH, 4)), dma((NCH, 4)),
            dma((3, NQ, 2)), dma((3, NQ, 2)),
            dma((NY * NQ,)), dma((NY,)),
            dma((4, 2)), dma((4, 2)),
            dma((2, NQ)), dma((2, NQ)),
            dma((3, 2, NQ)), dma((3, 2, NQ)),
            dma((2, 2)), dma((2, 2)),
            dma((NQ,)), dma((NQ,)),
        ],
        compiler_params=pltpu.CompilerParams(
            collective_id=0, has_side_effects=True, vmem_limit_bytes=56 * 2**20),
        name="panel_steps",
    )(factor.reshape(5, 2, T // 2, 2 * T), inverse.reshape(2, 2, 2, T // 2, T),
      rhs.reshape(5, T, NQ * W))
    return solved.reshape(rhs.shape)


def solution(mesh):
    return jax.shard_map(
        shards,
        mesh=mesh,
        in_specs=(P("row", "col"), P(None, "row", "col"), P("row", None)),
        out_specs=P("row", None),
        check_vma=False,
    )
```
